512 devices in a mesh: section: 16 (over y, core), seq: 8 (over z_lo, x), dp: 4 (over z_hi).
Axes of the slice: x: 4, y: 8, z: 8 (z_hi: 4, z_lo: 2; z = z_hi * 2 + z_lo), core: 2. Of those that a mesh axis runs over, the one named last changes fastest.
Arguments:
- hidden_in: bfloat16 [1, 4, 1024, 5120], P(None, 'dp', 'seq'), may hold values from -6 to 6
- out_grad: bfloat16 [1, 4, 1024, 2560], P(None, 'dp', 'seq'), may hold values from -6 to 6
- value_weight: bfloat16 [16, 5120, 512], P('section', 'dp'), may hold values from -0.078125 to 0.078125
- norm_gain: float32 [16, 5120], P('section'), may hold values from 0.25 to 1.75
Outputs:
- input_cov: float32 [16, 2560, 2560], P('section', 'seq', 'dp')
- output_cov: float32 [16, 512, 512], P('section', 'dp', 'seq')
The draws below stay inside these ranges and needn't reach their ends.
All inputs are finite; a program needn't handle non-finite values.
Results may differ from the reference program's by a relative error of at most 0.014.
Values may be sent and summed in bfloat16 or wider, within the bound.
A program may use at most 64 MiB of HBM per device.

```python
import jax
import jax.numpy as jnp
from jax import lax

D = 5120
HEAD = 128
GROUP = 5
MB = 1
KVW = 512
AW = 2560
LAYERS = 16
DOCS = 4
SEQLEN = 1024


def block_scale(key, shape, split, low, largest):
    gain = 1.0
    for dim, parts in split:
        steps = jax.random.uniform(jax.random.fold_in(jax.random.fold_in(key, 6), dim), (parts,), jnp.float32, low / len(split), largest / len(split))
        gain = gain * jnp.repeat(jnp.exp(steps), shape[dim] // parts).reshape((-1,) + (1,) * (len(shape) - 1 - dim))
    return gain


def bell_draw(key, shape, deviation, most, shards=(), kind=jnp.bfloat16):
    array = jax.random.normal(key, shape, jnp.float32) * deviation
    if len(shards) > 0:
        array = block_scale(key, shape, shards, -0.22, 0.18) * array
    return jnp.clip(array, min=-most, max=most).astype(kind)


def setup_inputs(seed: int = 0) -> dict:
    key_of = jax.random.split(jax.random.key(seed), 5)
    return {
        "hidden_in": bell_draw(key_of[0], (MB, DOCS, SEQLEN, D), 1.0, 6.0, ((1, 4), (2, 8))),
        "out_grad": bell_draw(key_of[1], (MB, DOCS, SEQLEN, AW), 1.0, 6.0, ((1, 4), (2, 8))),
        "value_weight": bell_draw(key_of[2], (LAYERS, D, KVW), D ** -0.5, 0.078125, ((0, 16), (1, 4))),
        "norm_gain": jnp.clip(1.0 + 0.15 * jax.random.normal(key_of[3], (LAYERS, D), jnp.float32), 0.25, 1.75),
    }


epsilon = 1e-06

def spread_heads(value_rows):
    row_count = value_rows.shape[0]
    shaped = value_rows.reshape(row_count, -1, 1, HEAD)
    return jnp.broadcast_to(shaped, (row_count, shaped.shape[1], GROUP, HEAD)).reshape(row_count, -1)

def collect_heads(grad_rows):
    row_count = grad_rows.shape[0]
    return lax.optimization_barrier(jnp.sum(grad_rows.reshape(row_count, -1, GROUP, HEAD), axis=2)).reshape(row_count, -1)

def reference(hidden_in, out_grad, value_weight, norm_gain):
    hidden = hidden_in.reshape(-1, D)
    rest_rows = hidden[:, AW:].astype(jnp.float32)
    window = hidden[:, :AW]
    token_count = hidden.shape[0]
    saved_rows = []
    input_list = []
    for layer_index in range(LAYERS):
        saved_rows.append(window)
        full_rows = jnp.concatenate([window.astype(jnp.float32), rest_rows], axis=1)
        inverse_rms = lax.rsqrt(lax.optimization_barrier(jnp.mean(full_rows * full_rows, axis=1, keepdims=True)) + epsilon)
        normed = (full_rows * inverse_rms * norm_gain[layer_index]).astype(jnp.bfloat16)
        head_rows = normed[:, :AW]
        input_list.append(jnp.dot(head_rows.T, head_rows, preferred_element_type=jnp.float32) / token_count)
        value_rows = jnp.dot(normed, value_weight[layer_index], preferred_element_type=jnp.float32)
        window = (window.astype(jnp.float32) + spread_heads(value_rows)).astype(jnp.bfloat16)
    grad_rows = out_grad.reshape(-1, AW)
    output_list = [None] * LAYERS
    for layer_index in range(LAYERS - 1, -1, -1):
        full_rows = jnp.concatenate([saved_rows[layer_index].astype(jnp.float32), rest_rows], axis=1)
        inverse_rms = lax.rsqrt(lax.optimization_barrier(jnp.mean(full_rows * full_rows, axis=1, keepdims=True)) + epsilon)
        dvalue = collect_heads(grad_rows.astype(jnp.float32)).astype(jnp.bfloat16)
        output_list[layer_index] = jnp.dot(dvalue.T, dvalue, preferred_element_type=jnp.float32) / token_count
        if layer_index > 0:
            dnormed = lax.dot_general(dvalue, value_weight[layer_index], (((1,), (1,)), ((), ())), preferred_element_type=jnp.float32)
            scaled = dnormed * norm_gain[layer_index]
            inner_mean = lax.optimization_barrier(jnp.mean(scaled * full_rows, axis=1, keepdims=True))
            change = inverse_rms * (scaled[:, :AW] - full_rows[:, :AW] * inverse_rms * inverse_rms * inner_mean)
            grad_rows = (grad_rows.astype(jnp.float32) + change).astype(jnp.bfloat16)
    return (jnp.stack(input_list), jnp.stack(output_list))
```

```python
import functools

import jax
import jax.numpy as jnp
from jax import lax
from jax.experimental import pallas as pl
from jax.experimental.pallas import tpu as pltpu
from jax.sharding import PartitionSpec as P

HEAD = 128
GROUP = 5
PARTS = 4
EARLY = 9

epsilon = 1e-06

MESH = pl.DeviceIdType.MESH
F32 = jnp.float32
BF16 = jnp.bfloat16


def remote(src, dst, send_sem, recv_sem, **device):
    return pltpu.make_async_remote_copy(
        src_ref=src,
        dst_ref=dst,
        send_sem=send_sem,
        recv_sem=recv_sem,
        device_id=device,
        device_id_type=MESH,
    )


def column(row):
    return jnp.transpose(jnp.broadcast_to(row, (128, 128)))


def kernel(
    token_count,
    hidden_ref,
    grad_ref,
    weight_ref,
    gain_ref,
    in_cov_ref,
    out_cov_ref,
    crossed,
    part_out,
    part_in,
    base,
    scaled,
    cmat,
    cmat_t,
    mean5,
    spare,
    state,
    state_out,
    product,
    inverse,
    inverse_row,
    inverse_in,
    grads,
    grad_out,
    hidden_in,
    rows_all,
    left_t,
    cov_out,
    cov_in,
    out_out,
    out_in,
    cross_sem,
    part_sem,
    cmat_send,
    cmat_recv,
    hidden_sem,
    forward_sem,
    backward_sem,
    state_sem,
    inverse_sem,
    grads_sem,
    cov_sem,
    out_sem,
):
    section = lax.axis_index("section")
    seq = lax.axis_index("seq")
    dp = lax.axis_index("dp")
    sections = lax.axis_size("section")
    seqs = lax.axis_size("seq")
    dps = lax.axis_size("dp")
    rows, width = hidden_ref.shape
    window = grad_ref.shape[1]
    depth, kvw = weight_ref.shape
    heads = kvw // HEAD
    step = rows // PARTS
    has_left = section > 0
    has_right = section < sections - 1

    barrier = pltpu.get_barrier_semaphore()
    for k in range(1, dps):
        pl.semaphore_signal(barrier, inc=1, device_id={"dp": (dp + k) % dps}, device_id_type=MESH)
    for j in range(1, seqs):
        pl.semaphore_signal(barrier, inc=1, device_id={"seq": seq ^ j}, device_id_type=MESH)

    @pl.when(has_left)
    def _():
        pl.semaphore_signal(barrier, inc=1, device_id={"section": section - 1}, device_id_type=MESH)

    @pl.when(has_right)
    def _():
        pl.semaphore_signal(barrier, inc=1, device_id={"section": section + 1}, device_id_type=MESH)

    pl.semaphore_wait(
        barrier, dps - 1 + seqs - 1 + has_left.astype(jnp.int32) + has_right.astype(jnp.int32)
    )

    def cross(k):
        other = (dp + k) % dps
        return remote(
            hidden_ref.at[:, pl.ds(pl.multiple_of(other * depth, 128), depth)],
            crossed.at[k - 1],
            cross_sem.at[0, k - 1],
            cross_sem.at[1, k - 1],
            dp=other,
        )

    def give_part(k):
        return remote(
            part_out.at[k - 1],
            part_in.at[k - 1],
            part_sem.at[0, k - 1],
            part_sem.at[1, k - 1],
            dp=(dp + dps - k) % dps,
        )

    def give_hidden(j):
        return remote(
            hidden_ref.at[:, pl.ds(0, window)],
            hidden_in.at[j - 1],
            hidden_sem.at[0, j - 1],
            hidden_sem.at[1, j - 1],
            seq=seq ^ j,
        )

    def give_state(j):
        return remote(
            state.at[pl.ds(0, rows)],
            state.at[pl.ds(j * rows, rows)],
            state_sem.at[0, j - 1],
            state_sem.at[1, j - 1],
            seq=seq ^ j,
        )

    def give_inverse(j):
        return remote(
            inverse_row,
            inverse_in.at[j - 1],
            inverse_sem.at[0, j - 1],
            inverse_sem.at[1, j - 1],
            seq=seq ^ j,
        )

    def give_grads(j):
        return remote(
            grads.at[pl.ds(0, rows)],
            grads.at[pl.ds(j * rows, rows)],
            grads_sem.at[0, j - 1],
            grads_sem.at[1, j - 1],
            seq=seq ^ j,
        )

    def give_cov(k):
        return remote(
            cov_out.at[k - 1],
            cov_in.at[k - 1],
            cov_sem.at[0, k - 1],
            cov_sem.at[1, k - 1],
            dp=(dp + k) % dps,
        )

    def give_out(k):
        return remote(
            out_out.at[k - 1],
            out_in.at[k - 1],
            out_sem.at[0, k - 1],
            out_sem.at[1, k - 1],
            dp=(dp + k) % dps,
        )

    half_rows = depth // GROUP

    def give_cmat(k, half):
        where = pl.ds(pl.multiple_of(half * half_rows, 16), half_rows)
        return remote(
            cmat.at[where], cmat.at[where], cmat_send.at[k - 1], cmat_recv.at[half], dp=(dp + k) % dps
        )

    for k in range(1, dps):
        cross(k).start()
    for j in range(1, seqs // 2):
        give_hidden(j).start()

    first = pl.multiple_of(dp * depth, 128)

    @pl.loop(0, depth // HEAD)
    def _(block):
        where = pl.ds(pl.multiple_of(block * HEAD, HEAD), HEAD)
        gain_here = column(gain_ref[:, pl.ds(pl.multiple_of(first + block * HEAD, HEAD), HEAD)])
        for c in range(kvw // 128):
            lanes = pl.ds(c * 128, 128)
            scaled[where, lanes] = (weight_ref[where, lanes].astype(F32) * gain_here).astype(BF16)

    halves = window // depth

    @pl.when(dp < halves)
    def _():
        for k in range(half_rows // HEAD):
            for c in range(kvw // 128):
                lanes = pl.ds(c * 128, 128)
                total = None
                for q in range(GROUP):
                    block = (k * GROUP + q) * HEAD
                    gain_here = column(
                        gain_ref[:, pl.ds(pl.multiple_of(first + block, HEAD), HEAD)]
                    )
                    term = weight_ref[pl.ds(block, HEAD), lanes].astype(F32) * gain_here
                    total = term if total is None else total + term
                cmat[pl.ds(pl.multiple_of(dp * half_rows + k * HEAD, 16), HEAD), lanes] = (
                    total.astype(BF16)
                )
        for k in range(1, dps):
            give_cmat(k, dp).start()

    fixed = jnp.zeros((rows, HEAD), F32)
    for k in range(heads):
        parts = [
            hidden_ref[:, pl.ds((k * GROUP + q) * HEAD, HEAD)].astype(F32) for q in range(GROUP)
        ]
        mean = (parts[0] + parts[1] + parts[2] + parts[3] + parts[4]) * (1.0 / GROUP)
        mean5[:, pl.ds(k * HEAD, HEAD)] = mean
        for part in parts:
            fixed = fixed + (part - mean) * (part - mean)
    for b in range(window // HEAD, width // HEAD):
        part = hidden_ref[:, pl.ds(b * HEAD, HEAD)].astype(F32)
        fixed = fixed + part * part
    spare[...] = jnp.broadcast_to(jnp.sum(fixed, axis=1, keepdims=True), (rows, 128))

    @pl.when(section == 0)
    def _():
        state[pl.ds(0, rows), :] = jnp.zeros((rows, kvw), BF16)

    @pl.when(section == sections - 1)
    def _():
        for k in range(heads):
            total = grad_ref[:, pl.ds(k * GROUP * HEAD, HEAD)].astype(F32)
            for q in range(1, GROUP):
                total = total + grad_ref[:, pl.ds((k * GROUP + q) * HEAD, HEAD)].astype(F32)
            grads[pl.ds(0, rows), pl.ds(k * HEAD, HEAD)] = total.astype(BF16)

    base[...] = jnp.dot(
        hidden_ref[:, pl.ds(first, depth)], scaled[...], preferred_element_type=F32
    )
    for k in (1, 3, 2):
        cross(k).wait_recv()
        part_out[k - 1] = jnp.dot(
            crossed[k - 1], scaled[...], preferred_element_type=F32
        ).astype(BF16)
        give_part(k).start()
    for half in range(halves):

        @pl.when(dp != half)
        def _():
            give_cmat(1, half).wait_recv()

    cmat_t[...] = jnp.transpose(cmat[...])
    for k in (1, 3, 2):
        give_part(k).wait_recv()
        base[...] += part_in[k - 1].astype(F32)
    for j in range(seqs // 2, seqs):
        give_hidden(j).start()

    def send_forward(i):
        where = pl.ds(i * step, step)
        return remote(
            state_out.at[where],
            state.at[where],
            forward_sem.at[0, i],
            forward_sem.at[1, i],
            section=section + 1,
        )

    def send_backward(i):
        where = pl.ds(i * step, step)
        return remote(
            grad_out.at[where],
            grads.at[where],
            backward_sem.at[0, i],
            backward_sem.at[1, i],
            section=section - 1,
        )

    for i in range(PARTS):
        where = pl.ds(i * step, step)

        @pl.when(has_left)
        def _():
            send_forward(i).wait_recv()

        s = state[where, :]
        s32 = s.astype(F32)
        x = s32 + mean5[where, :]
        squares = spare[where, 0:1] + GROUP * jnp.sum(x * x, axis=1, keepdims=True)
        inv = lax.rsqrt(squares * (1.0 / width) + epsilon)
        prod = jnp.dot(s, cmat[...], preferred_element_type=F32) + base[where, :]
        state_out[where, :] = (s32 + inv * prod).astype(BF16)

        @pl.when(has_right)
        def _():
            send_forward(i).start()

        product[where, :] = prod
        inverse[where, :] = jnp.broadcast_to(inv, (step, 128))

    inverse_row[...] = jnp.transpose(inverse[...])[0:8, :]
    for j in range(1, seqs):
        give_state(j).start()
        give_inverse(j).start()

    def backward():
        for i in range(PARTS):
            where = pl.ds(i * step, step)

            @pl.when(has_right)
            def _():
                send_backward(i).wait_recv()

            @pl.when(has_left)
            def _():
                g = grads[where, :]
                g32 = g.astype(F32)
                turned = jnp.dot(g, cmat_t[...], preferred_element_type=F32)
                inner = jnp.sum(g32 * product[where, :], axis=1, keepdims=True) * (1.0 / width)
                inv = inverse[where, 0:1]
                x = state[where, :].astype(F32) + mean5[where, :]
                change = inv * (turned - x * (GROUP * inv * inv * inner))
                grad_out[where, :] = (g32 + change).astype(BF16)
                send_backward(i).start()

        for j in range(1, seqs):
            give_grads(j).start()

    start = pl.multiple_of((seq // 2) * (GROUP * HEAD) + (seq % 2) * 256, 128)
    odd = seq % 2
    block_rows = in_cov_ref.shape[0]
    block_cols = in_cov_ref.shape[1]

    def fill(j, read_hidden, inv):
        here = pl.ds(j * rows, rows)
        for k in range(heads):
            s32 = state[here, pl.ds(k * HEAD, HEAD)].astype(F32)
            for q in range(GROUP):
                lanes = pl.ds((k * GROUP + q) * HEAD, HEAD)
                rows_all[here, lanes] = (read_hidden(lanes).astype(F32) + s32).astype(BF16)
        factor = inv * inv
        for c in range(3):
            lanes = pl.ds(pl.multiple_of(start + c * 128, 128), 128)
            part = rows_all[here, lanes].astype(F32) * factor * gain_ref[:, lanes]
            left_t[pl.ds(c * 128, 128), here] = jnp.transpose(part).astype(BF16)

    def input_cov():
        fill(0, lambda lanes: hidden_ref[:, lanes], inverse[...])
        for j in range(1, seqs):
            give_hidden(j).wait_recv()
            give_state(j).wait_recv()
            give_inverse(j).wait_recv()
            fill(j, lambda lanes: hidden_in[j - 1, :, lanes], column(inverse_in[j - 1, 0:1, :]))

        def block(other):
            lanes = pl.ds(pl.multiple_of(other * block_cols, 128), block_cols)
            part = jnp.dot(left_t[...], rows_all[:, lanes], preferred_element_type=F32)
            part = part * gain_ref[:, lanes]
            return jnp.where(odd == 0, part[:block_rows], part[64 : 64 + block_rows])

        for k in (2, 1, 3):
            cov_out[k - 1] = block((dp + k) % dps).astype(BF16)
            give_cov(k).start()
        in_cov_ref[...] = block(dp)

    early = section <= EARLY

    @pl.loop(0, 2)
    def _(phase):
        @pl.when((phase == 0) == early)
        def _():
            input_cov()

        @pl.when((phase == 0) != early)
        def _():
            backward()

    for j in range(1, seqs):
        give_grads(j).wait_recv()
    lanes = pl.ds(pl.multiple_of((seq // 2) * 128, 128), 128)
    left = jnp.transpose(grads[:, lanes])
    turned = jnp.dot(left, grads[...], preferred_element_type=F32)
    out_parts = [turned[:, b * HEAD : (b + 1) * HEAD] for b in range(dps)]

    def pick(other):
        part = out_parts[0]
        for b in range(1, dps):
            part = jnp.where(other == b, out_parts[b], part)
        return part

    for k in range(1, dps):
        out_out[k - 1] = pick((dp + k) % dps).astype(BF16)
        give_out(k).start()
    own = pick(dp)

    total = in_cov_ref[...]
    for k in (1, 3, 2):
        give_cov(k).wait_recv()
        total = total + cov_in[k - 1].astype(F32)
    in_cov_ref[...] = total * (1.0 / token_count)

    for k in (1, 3, 2):
        give_out(k).wait_recv()
        own = own + out_in[k - 1].astype(F32)
    own = jnp.transpose(own) * (1.0 / token_count)
    out_cov_ref[...] = jnp.where(odd == 0, own[:, :64], own[:, 64:])

    for k in range(1, dps):
        cross(k).wait_send()
        give_part(k).wait_send()
        give_cov(k).wait_send()
        give_out(k).wait_send()
    for j in range(1, seqs):
        give_hidden(j).wait_send()
        give_state(j).wait_send()
        give_inverse(j).wait_send()
        give_grads(j).wait_send()

    @pl.when(dp < halves)
    def _():
        for k in range(1, dps):
            give_cmat(k, dp).wait_send()

    @pl.when(has_right)
    def _():
        for i in range(PARTS):
            send_forward(i).wait_send()

    @pl.when(has_left)
    def _():
        for i in range(PARTS):
            send_backward(i).wait_send()


def on_device(hidden_in, out_grad, value_weight, norm_gain):
    seqs = lax.axis_size("seq")
    dps = lax.axis_size("dp")
    rows, width = hidden_in.shape[2:]
    window = out_grad.shape[3]
    depth, kvw = value_weight.shape[1:]
    token_count = rows * seqs * dps
    block = (window // seqs, window // dps)
    out_block = (kvw // dps, kvw // seqs)
    half_rows = depth // GROUP
    dma = pltpu.SemaphoreType.DMA
    vmem = pl.BlockSpec(memory_space=pltpu.VMEM)
    scratch = [
        pltpu.VMEM((dps - 1, rows, depth), BF16),
        pltpu.VMEM((dps - 1, rows, kvw), BF16),
        pltpu.VMEM((dps - 1, rows, kvw), BF16),
        pltpu.VMEM((rows, kvw), F32),
        pltpu.VMEM((depth, kvw), BF16),
        pltpu.VMEM((kvw, kvw), BF16),
        pltpu.VMEM((kvw, kvw), BF16),
        pltpu.VMEM((rows, kvw), F32),
        pltpu.VMEM((rows, 128), F32),
        pltpu.VMEM((seqs * rows, kvw), BF16),
        pltpu.VMEM((rows, kvw), BF16),
        pltpu.VMEM((rows, kvw), F32),
        pltpu.VMEM((rows, 128), F32),
        pltpu.VMEM((8, rows), F32),
        pltpu.VMEM((seqs - 1, 8, rows), F32),
        pltpu.VMEM((seqs * rows, kvw), BF16),
        pltpu.VMEM((rows, kvw), BF16),
        pltpu.VMEM((seqs - 1, rows, window), BF16),
        pltpu.VMEM((seqs * rows, window), BF16),
        pltpu.VMEM((384, seqs * rows), BF16),
        pltpu.VMEM((dps - 1,) + block, BF16),
        pltpu.VMEM((dps - 1,) + block, BF16),
        pltpu.VMEM((dps - 1, HEAD, 128), BF16),
        pltpu.VMEM((dps - 1, HEAD, 128), BF16),
        dma((2, dps - 1)),
        dma((2, dps - 1)),
        dma((dps - 1,)),
        dma((window // depth,)),
        dma((2, seqs - 1)),
        dma((2, PARTS)),
        dma((2, PARTS)),
        dma((2, seqs - 1)),
        dma((2, seqs - 1)),
        dma((2, seqs - 1)),
        dma((2, dps - 1)),
        dma((2, dps - 1)),
    ]
    input_cov, output_cov = pl.pallas_call(
        functools.partial(kernel, token_count),
        out_shape=(
            jax.ShapeDtypeStruct(block, F32),
            jax.ShapeDtypeStruct(out_block, F32),
        ),
        in_specs=[vmem] * 4,
        out_specs=(vmem, vmem),
        scratch_shapes=scratch,
        compiler_params=pltpu.CompilerParams(
            collective_id=0, has_side_effects=True, vmem_limit_bytes=56 * 1024 * 1024
        ),
    )(
        hidden_in.reshape(rows, width),
        out_grad.reshape(rows, window),
        value_weight.reshape(depth, kvw),
        norm_gain,
    )
    return (input_cov[None], output_cov[None])


def solution(mesh):
    return jax.shard_map(
        on_device,
        mesh=mesh,
        in_specs=(
            P(None, "dp", "seq", None),
            P(None, "dp", "seq", None),
            P("section", "dp", None),
            P("section", None),
        ),
        out_specs=(P("section", "seq", "dp"), P("section", "dp", "seq")),
        check_vma=False,
    )
```

```python
import functools

import jax
import jax.numpy as jnp
from jax import lax
from jax.experimental import pallas as pl
from jax.experimental.pallas import tpu as pltpu
from jax.sharding import PartitionSpec as P

HEAD = 128
GROUP = 5
CORES = 2
RING = 4
PARTS = 2
EARLY = 4

epsilon = 1e-06

MESH = pl.DeviceIdType.MESH
F32 = jnp.float32
BF16 = jnp.bfloat16


def column(row):
    return jnp.transpose(jnp.broadcast_to(row, (128, 128)))


def kernel(
    token_count,
    hidden_ref,
    grad_ref,
    weight_ref,
    gain_ref,
    in_cov_ref,
    out_cov_ref,
    crossed,
    relayed,
    gain_col,
    scaled,
    cmat,
    cmat_t,
    mean5,
    spare,
    own_out,
    own_in,
    far_out,
    far_in,
    near_out,
    near_in,
    base,
    chain_in,
    chain_out,
    centred,
    product,
    inverse,
    states,
    state,
    inverse_all,
    inverse_row,
    inverse_in,
    grad_in,
    grad_out,
    dvalues,
    grads,
    hidden_in,
    rows_all,
    left_t,
    cov_far,
    cov_relay,
    cov_near,
    cov_in,
    left_g,
    turned,
    out_send,
    out_recv,
    cross_sem,
    relay_sem,
    share_sem,
    cmat_sem,
    fold_sem,
    own_sem,
    far_sem,
    near_sem,
    chain_sem,
    lend_sem,
    hidden_sem,
    hidden_share,
    state_sem,
    inverse_sem,
    grads_sem,
    cov_sem,
    out_sem,
):
    section = lax.axis_index("section")
    seq = lax.axis_index("seq")
    dp = lax.axis_index("dp")
    sections = lax.axis_size("section")
    seqs = lax.axis_size("seq")
    dps = lax.axis_size("dp")
    rows, width = hidden_ref.shape
    window = grad_ref.shape[1]
    depth, kvw = weight_ref.shape
    heads = kvw // HEAD
    chip = section // CORES
    core = section % CORES
    sibling = chip * CORES + (1 - core)
    has_left = chip > 0
    has_right = chip < sections // CORES - 1
    x = seq % RING
    z_low = seq // RING
    x_next = z_low * RING + (x + 1) % RING
    x_last = z_low * RING + (x + RING - 1) % RING
    z_pair = (1 - z_low) * RING + x
    dp_next = (dp + 1) % dps
    dp_last = (dp + dps - 1) % dps
    half = rows // CORES
    step = half // PARTS

    sent = []

    def remote(src, dst, sem, *index, **device):
        return pltpu.make_async_remote_copy(
            src_ref=src,
            dst_ref=dst,
            send_sem=sem.at[(0,) + index],
            recv_sem=sem.at[(1,) + index],
            device_id=device,
            device_id_type=MESH,
        )

    def start(copy):
        copy.start()
        sent.append(copy)

    barrier = pltpu.get_barrier_semaphore()

    def greet(**device):
        pl.semaphore_signal(barrier, inc=1, device_id=device, device_id_type=MESH)

    for k in range(1, dps):
        greet(dp=(dp + k) % dps)
        greet(dp=(dp + k) % dps, seq=z_pair)
    for j in range(1, seqs):
        greet(seq=seq ^ j)
    greet(section=sibling)
    greet(section=sibling, dp=dp_next)
    greet(section=sibling, dp=dp_last)

    @pl.when(has_left)
    def _():
        greet(section=section - CORES)

    @pl.when(has_right)
    def _():
        greet(section=section + CORES)

    pl.semaphore_wait(
        barrier,
        2 * (dps - 1) + seqs - 1 + 3 + has_left.astype(jnp.int32) + has_right.astype(jnp.int32),
    )

    piece = depth // CORES
    my_piece = pl.ds(pl.multiple_of(core * piece, 128), piece)

    def columns_of(other):
        return pl.ds(pl.multiple_of(other * depth + core * piece, 128), piece)

    def cross(k):
        if k == 0:
            return remote(
                hidden_ref.at[:, columns_of(dp_next)],
                crossed.at[0, :, my_piece],
                cross_sem,
                0,
                dp=dp_next,
            )
        return remote(
            hidden_ref.at[:, columns_of(dp_last)],
            crossed.at[2, :, my_piece],
            cross_sem,
            1,
            dp=dp_last,
        )

    far_columns = columns_of((dp + 2) % dps)

    def far_first(k):
        return remote(
            hidden_ref.at[pl.ds(k * half, half), far_columns],
            relayed.at[k],
            relay_sem,
            k,
            dp=dp_next if k == 0 else dp_last,
        )

    def far_second(k):
        return remote(
            relayed.at[k],
            crossed.at[1, pl.ds(k * half, half), my_piece],
            relay_sem,
            2 + k,
            dp=dp_next if k == 0 else dp_last,
        )

    def share(slot):
        return remote(
            crossed.at[slot, :, my_piece],
            crossed.at[slot, :, my_piece],
            share_sem,
            slot,
            section=sibling,
        )

    start(far_first(0))
    start(far_first(1))
    start(cross(0))
    start(cross(1))

    first = pl.multiple_of(dp * depth, 128)

    @pl.loop(0, depth // HEAD)
    def _(block):
        where = pl.ds(pl.multiple_of(block * HEAD, HEAD), HEAD)
        gain_here = column(gain_ref[:, pl.ds(pl.multiple_of(first + block * HEAD, HEAD), HEAD)])
        gain_col[where, :] = gain_here
        for c in range(kvw // 128):
            lanes = pl.ds(c * 128, 128)
            scaled[where, lanes] = (weight_ref[where, lanes].astype(F32) * gain_here).astype(BF16)

    halves = window // depth
    fold_rows = kvw // halves
    chunk = fold_rows // seqs
    fold_here = pl.ds(pl.multiple_of(seq * chunk, 16), chunk)

    def give_fold(k, part):
        where = cmat.at[core, part, fold_here]
        return pltpu.make_async_remote_copy(
            src_ref=where,
            dst_ref=where,
            send_sem=fold_sem.at[0, k - 1],
            recv_sem=fold_sem.at[1, part],
            device_id={"dp": (dp + k) % dps},
            device_id_type=MESH,
        )

    def give_cmat(j):
        where = cmat.at[core, :, fold_here]
        return remote(where, where, cmat_sem, j - 1, seq=seq ^ j)

    def share_cmat():
        return remote(cmat.at[core], cmat.at[core], cmat_sem, seqs - 1, section=sibling)

    @pl.when(dp < halves)
    def _():
        per_head = HEAD // chunk
        row = (seq // per_head) * (GROUP * HEAD) + (seq % per_head) * chunk
        for c in range(kvw // 128):
            lanes = pl.ds(c * 128, 128)
            total = None
            for q in range(GROUP):
                where = pl.ds(pl.multiple_of(row + q * HEAD, 16), chunk)
                term = weight_ref[where, lanes].astype(F32) * gain_col[where, :]
                total = term if total is None else total + term
            cmat[core, dp, fold_here, lanes] = total.astype(BF16)
        for k in range(1, dps):
            give_fold(k, dp).start()

    def give_own():
        return remote(
            own_out.at[pl.ds(pl.multiple_of((1 - core) * half, 16), half)],
            own_in,
            own_sem,
            section=sibling,
        )

    own_out[...] = jnp.dot(
        hidden_ref[:, pl.ds(first, depth)], scaled[...], preferred_element_type=F32
    )
    start(give_own())

    for part in range(halves):

        @pl.when(dp != part)
        def _():
            give_fold(1, part).wait_recv()

    for j in range(1, seqs):
        start(give_cmat(j))

    def ring(sem, view):
        front, back = (0, half), (half, half)
        full = (0, rows)
        plan = (
            (0, 4, full, z_pair),
            (0, 1, full, x_next),
            (0, 2, full, x_last),
            (4, 5, full, x_next),
            (4, 6, full, x_last),
            (1, 3, front, x_next),
            (2, 3, back, x_last),
            (5, 7, front, x_next),
            (6, 7, back, x_last),
        )

        def copy(i):
            src, dst, part, device = plan[i]
            return remote(view(src, *part), view(dst, *part), sem, i, seq=device)

        return copy

    wide = window // CORES
    my_wide = pl.ds(pl.multiple_of(core * wide, 128), wide)

    def hidden_view(slot, low, count):
        if slot == 0:
            return hidden_ref.at[pl.ds(low, count), my_wide]
        return hidden_in.at[slot - 1, pl.ds(low, count), my_wide]

    def share_hidden(slot):
        where = hidden_in.at[slot - 1, :, my_wide]
        return remote(where, where, hidden_share, slot - 1, section=sibling)

    give_hidden = ring(hidden_sem, hidden_view)
    give_state = ring(state_sem, lambda slot, low, count: state.at[pl.ds(slot * rows + low, count)])
    give_grads = ring(grads_sem, lambda slot, low, count: grads.at[pl.ds(slot * rows + low, count)])

    def give_inverse(slot):
        z_there = z_low if slot < RING else 1 - z_low
        x_there = (x + (0, 1, 3, 2)[slot % RING]) % RING
        return remote(
            inverse_row,
            inverse_in.at[slot - 1],
            inverse_sem,
            slot - 1,
            seq=z_there * RING + x_there,
        )

    start(give_hidden(1))
    start(give_hidden(2))

    for k in range(2):
        far_first(k).wait_recv()
        start(far_second(k))

    fixed = jnp.zeros((rows, HEAD), F32)
    for k in range(heads):
        parts = [
            hidden_ref[:, pl.ds((k * GROUP + q) * HEAD, HEAD)].astype(F32) for q in range(GROUP)
        ]
        mean = (parts[0] + parts[1] + parts[2] + parts[3] + parts[4]) * (1.0 / GROUP)
        mean5[:, pl.ds(k * HEAD, HEAD)] = mean
        for part in parts:
            fixed = fixed + (part - mean) * (part - mean)
    for b in range(window // HEAD, width // HEAD):
        part = hidden_ref[:, pl.ds(b * HEAD, HEAD)].astype(F32)
        fixed = fixed + part * part
    spare[...] = jnp.broadcast_to(jnp.sum(fixed, axis=1, keepdims=True), (rows, 128))

    my_rows = pl.ds(pl.multiple_of(core * half, 16), half)

    @pl.when(chip == 0)
    def _():
        chain_in[...] = jnp.zeros((half, kvw), BF16)

    @pl.when(jnp.logical_not(has_right))
    def _():
        for k in range(heads):
            total = grad_ref[my_rows, pl.ds(k * GROUP * HEAD, HEAD)].astype(F32)
            for q in range(1, GROUP):
                total = total + grad_ref[my_rows, pl.ds((k * GROUP + q) * HEAD, HEAD)].astype(F32)
            grad_in[:, pl.ds(k * HEAD, HEAD)] = total.astype(BF16)

    cross(0).wait_recv()
    start(share(0))
    cross(1).wait_recv()
    start(share(2))
    for k in range(2):
        far_second(k).wait_recv()
    start(share(1))

    def partial_rows(slot):
        share(slot).wait_recv()
        return jnp.dot(crossed[slot], scaled[...], preferred_element_type=F32)

    def give_far(k):
        return remote(
            far_out.at[pl.ds(k * half, half)],
            far_in.at[k],
            far_sem,
            k,
            dp=dp_next if k == 0 else dp_last,
        )

    def give_near(way, other_core):
        return remote(
            near_out.at[way, pl.ds(other_core * half, half)],
            near_in.at[core, way],
            near_sem,
            core,
            way,
            other_core,
            dp=dp_next if way == 0 else dp_last,
            section=chip * CORES + other_core,
        )

    def near_arrived(layer, way):
        where = near_in.at[layer, way]
        pltpu.make_async_remote_copy(
            src_ref=where,
            dst_ref=where,
            send_sem=near_sem.at[0, layer, way, core],
            recv_sem=near_sem.at[1, layer, way, core],
            device_id={"dp": dp_next},
            device_id_type=MESH,
        ).wait_recv()

    far_out[...] = partial_rows(1).astype(BF16)
    start(give_far(0))
    start(give_far(1))
    near_next = partial_rows(2)
    near_out[0, pl.ds(half, half), :] = near_next[half:].astype(BF16)
    start(give_near(0, 1))
    near_last = partial_rows(0)
    near_out[1, pl.ds(0, half), :] = near_last[:half].astype(BF16)
    start(give_near(1, 0))
    give_far(0).wait_recv()
    near_out[0, pl.ds(0, half), :] = (near_next[:half] + far_in[0].astype(F32)).astype(BF16)
    start(give_near(0, 0))
    give_far(1).wait_recv()
    near_out[1, pl.ds(half, half), :] = (near_last[half:] + far_in[1].astype(F32)).astype(BF16)
    start(give_near(1, 1))

    for j in range(1, seqs):
        give_cmat(j).wait_recv()
    start(share_cmat())
    share_cmat().wait_recv()
    for layer in range(CORES):
        cmat_t[layer] = jnp.transpose(cmat[layer].reshape(kvw, kvw))

    give_hidden(1).wait_recv()
    start(give_hidden(5))
    start(share_hidden(1))
    give_hidden(2).wait_recv()
    start(give_hidden(6))
    start(share_hidden(2))

    give_own().wait_recv()
    for layer in range(CORES):
        near_arrived(layer, 0)
        near_arrived(layer, 1)
        own = jnp.where(core == layer, own_out[my_rows, :], own_in[...])
        base[layer] = own + (near_in[layer, 0].astype(F32) + near_in[layer, 1].astype(F32))
    start(give_hidden(0))

    def send_forward(i):
        where = pl.ds(i * step, step)
        return remote(
            chain_out.at[where], chain_in.at[where], chain_sem, 0, i, section=section + CORES
        )

    def send_backward(i):
        where = pl.ds(i * step, step)
        return remote(
            grad_out.at[where], grad_in.at[where], chain_sem, 1, i, section=section - CORES
        )

    for i in range(PARTS):
        where = pl.ds(i * step, step)
        here = pl.ds(pl.multiple_of(core * half + i * step, 16), step)

        @pl.when(has_left)
        def _():
            send_forward(i).wait_recv()

        s = chain_in[where, :]
        s32 = s.astype(F32)
        for layer in range(CORES):
            c32 = s32 + mean5[here, :]
            squares = spare[here, 0:1] + GROUP * jnp.sum(c32 * c32, axis=1, keepdims=True)
            inv = lax.rsqrt(squares * (1.0 / width) + epsilon)
            prod = (
                jnp.dot(s, cmat[layer].reshape(kvw, kvw), preferred_element_type=F32)
                + base[layer, where, :]
            )
            states[layer, where, :] = s
            centred[layer, where, :] = c32
            product[layer, where, :] = prod
            inverse[layer, where, :] = jnp.broadcast_to(inv, (step, 128))
            s32 = s32 + inv * prod
            s = s32.astype(BF16)
        chain_out[where, :] = s

        @pl.when(has_right)
        def _():
            send_forward(i).start()

    def lend_state():
        return remote(states.at[1 - core], state.at[my_rows], lend_sem, 0, section=sibling)

    def lend_inverse():
        return remote(inverse.at[1 - core], inverse_all.at[my_rows], lend_sem, 1, section=sibling)

    def lend_grads():
        return remote(dvalues.at[1 - core], grads.at[my_rows], lend_sem, 2, section=sibling)

    start(lend_state())
    start(lend_inverse())
    state[my_rows, :] = states[core]
    inverse_all[my_rows, :] = inverse[core]
    lend_state().wait_recv()
    for i in range(3):
        start(give_state(i))
    lend_inverse().wait_recv()
    inverse_row[...] = jnp.transpose(inverse_all[...])[0:8, :]
    for slot in range(1, seqs):
        start(give_inverse(slot))
    give_hidden(0).wait_recv()
    start(give_hidden(3))
    start(give_hidden(4))
    start(share_hidden(4))

    def backward():
        for i in range(PARTS):
            where = pl.ds(i * step, step)

            @pl.when(has_right)
            def _():
                send_backward(i).wait_recv()

            def turn(g, g32, layer):
                other = jnp.dot(g, cmat_t[layer], preferred_element_type=F32)
                inner = jnp.sum(g32 * product[layer, where, :], axis=1, keepdims=True)
                inv = inverse[layer, where, 0:1]
                factor = inv * inv * inner * (GROUP / width)
                return g32 + inv * (other - centred[layer, where, :] * factor)

            g = grad_in[where, :]
            dvalues[1, where, :] = g
            g32 = turn(g, g.astype(F32), 1)
            g = g32.astype(BF16)
            dvalues[0, where, :] = g

            @pl.when(has_left)
            def _():
                grad_out[where, :] = turn(g, g.astype(F32), 0).astype(BF16)
                send_backward(i).start()

        lend_grads().start()
        grads[my_rows, :] = dvalues[core]
        lend_grads().wait_recv()
        for i in (1, 2):
            give_grads(i).start()

    begin = pl.multiple_of((seq // 2) * (GROUP * HEAD) + (seq % 2) * 256, 128)
    odd = seq % 2
    block_rows, block_cols = in_cov_ref.shape
    cov_half = block_rows // 2

    def fill(slot, read_hidden, inv):
        here = pl.ds(slot * rows, rows)
        for k in range(heads):
            s32 = state[here, pl.ds(k * HEAD, HEAD)].astype(F32)
            for q in range(GROUP):
                lanes = pl.ds((k * GROUP + q) * HEAD, HEAD)
                rows_all[here, lanes] = (read_hidden(lanes).astype(F32) + s32).astype(BF16)
        factor = inv * inv
        for c in range(3):
            lanes = pl.ds(pl.multiple_of(begin + c * 128, 128), 128)
            part = rows_all[here, lanes].astype(F32) * factor * gain_ref[:, lanes]
            left_t[pl.ds(c * 128, 128), here] = jnp.transpose(part).astype(BF16)

    def give_cov_far(k):
        return remote(
            cov_far.at[pl.ds(k * cov_half, cov_half)],
            cov_relay.at[k],
            cov_sem,
            k,
            dp=dp_next if k == 0 else dp_last,
        )

    def give_cov(k):
        return remote(
            cov_near.at[k], cov_in.at[k], cov_sem, 2 + k, dp=dp_next if k == 0 else dp_last
        )

    def input_cov():
        def take(slot):
            share_hidden(slot).wait_recv()
            give_inverse(slot).wait_recv()
            fill(
                slot,
                lambda lanes: hidden_in[slot - 1, :, lanes],
                column(inverse_in[slot - 1, 0:1, :]),
            )

        give_state(0).wait_recv()
        give_state(3).start()
        give_state(4).start()
        give_state(1).wait_recv()
        give_state(5).start()
        give_state(2).wait_recv()
        give_state(6).start()
        give_hidden(3).wait_recv()
        give_hidden(7).start()
        share_hidden(5).start()
        give_hidden(4).wait_recv()
        give_hidden(8).start()
        share_hidden(6).start()
        give_hidden(5).wait_recv()
        give_hidden(6).wait_recv()
        share_hidden(3).start()
        fill(0, lambda lanes: hidden_ref[:, lanes], inverse_all[...])
        take(1)
        give_state(3).wait_recv()
        give_state(7).start()
        give_state(4).wait_recv()
        give_state(8).start()
        take(2)
        take(4)
        give_hidden(7).wait_recv()
        give_hidden(8).wait_recv()
        share_hidden(7).start()
        give_state(5).wait_recv()
        give_state(6).wait_recv()
        take(3)
        take(5)
        take(6)
        give_state(7).wait_recv()
        give_state(8).wait_recv()
        take(7)

        def block(other):
            lanes = pl.ds(pl.multiple_of(other * block_cols, 128), block_cols)
            part = jnp.dot(left_t[...], rows_all[:, lanes], preferred_element_type=F32)
            part = part * gain_ref[:, lanes]
            return jnp.where(odd == 0, part[:block_rows], part[64 : 64 + block_rows])

        cov_far[...] = block((dp + 2) % dps).astype(BF16)
        give_cov_far(0).start()
        give_cov_far(1).start()
        in_cov_ref[...] = block(dp)
        part = block(dp_next)
        cov_near[0, pl.ds(cov_half, cov_half), :] = part[cov_half:].astype(BF16)
        give_cov_far(0).wait_recv()
        cov_near[0, pl.ds(0, cov_half), :] = (
            part[:cov_half] + cov_relay[0].astype(F32)
        ).astype(BF16)
        give_cov(0).start()
        part = block(dp_last)
        cov_near[1, pl.ds(0, cov_half), :] = part[:cov_half].astype(BF16)
        give_cov_far(1).wait_recv()
        cov_near[1, pl.ds(cov_half, cov_half), :] = (
            part[cov_half:] + cov_relay[1].astype(F32)
        ).astype(BF16)
        give_cov(1).start()

    early = chip <= EARLY

    @pl.loop(0, 2)
    def _(phase):
        @pl.when((phase == 0) == early)
        def _():
            input_cov()

        @pl.when((phase == 0) != early)
        def _():
            backward()

    give_grads(1).wait_recv()
    start(give_grads(5))
    give_grads(2).wait_recv()
    start(give_grads(6))
    out_rows = out_cov_ref.shape[0]
    for z in range(2):
        lanes = pl.ds(pl.multiple_of(z * (kvw // 2) + (x // 2) * 128, 128), 128)
        for slot in range(3):
            here = pl.ds(slot * rows, rows)
            left_g[z, :, here] = jnp.transpose(grads[here, lanes].astype(F32)).astype(BF16)
    give_grads(5).wait_recv()
    give_grads(6).wait_recv()
    for z in range(2):
        lanes = pl.ds(pl.multiple_of(z * (kvw // 2) + (x // 2) * 128, 128), 128)
        here = pl.ds(3 * rows, rows)
        left_g[z, :, here] = jnp.transpose(grads[here, lanes].astype(F32)).astype(BF16)
        mine = pl.ds(pl.multiple_of((x % 2) * out_rows, 16), out_rows)
        turned[z] = jnp.dot(
            left_g[z, mine, :], grads[pl.ds(0, RING * rows), :], preferred_element_type=F32
        )

    def block_of(k):
        z = z_low if k % 2 == 0 else 1 - z_low
        lanes = pl.ds(pl.multiple_of(((dp + k // 2) % dps) * HEAD, 128), HEAD)
        return turned[z, :, lanes]

    def give_out(k):
        return remote(
            out_send.at[k - 1],
            out_recv.at[k - 1],
            out_sem,
            k - 1,
            dp=(dp + k // 2) % dps,
            seq=seq if k % 2 == 0 else z_pair,
        )

    for k in range(1, 2 * dps):
        out_send[k - 1] = block_of(k).astype(BF16)
        start(give_out(k))

    total = in_cov_ref[...]
    for k in range(2):
        give_cov(k).wait_recv()
        total = total + cov_in[k].astype(F32)
    in_cov_ref[...] = total * (1.0 / token_count)

    own = block_of(0)
    for k in range(1, 2 * dps):
        give_out(k).wait_recv()
        own = own + out_recv[k - 1].astype(F32)
    out_cov_ref[...] = own * (1.0 / token_count)

    for copy in sent:
        copy.wait_send()
    for slot in (3, 5, 6, 7):
        share_hidden(slot).wait_send()
    for i in (7, 8):
        give_hidden(i).wait_send()
    for i in range(3, 9):
        give_state(i).wait_send()
    for i in (1, 2):
        give_grads(i).wait_send()
    lend_grads().wait_send()
    for k in range(2):
        give_cov_far(k).wait_send()
        give_cov(k).wait_send()

    @pl.when(dp < halves)
    def _():
        for k in range(1, dps):
            give_fold(k, dp).wait_send()

    @pl.when(has_right)
    def _():
        for i in range(PARTS):
            send_forward(i).wait_send()

    @pl.when(has_left)
    def _():
        for i in range(PARTS):
            send_backward(i).wait_send()


def on_device(hidden_in, out_grad, value_weight, norm_gain):
    seqs = lax.axis_size("seq")
    dps = lax.axis_size("dp")
    rows, width = hidden_in.shape[2:]
    window = out_grad.shape[3]
    depth, kvw = value_weight.shape[1:]
    token_count = rows * seqs * dps
    half = rows // CORES
    block = (window // seqs, window // dps)
    out_block = (kvw // seqs, kvw // dps)
    halves = window // depth
    dma = pltpu.SemaphoreType.DMA
    vmem = pl.BlockSpec(memory_space=pltpu.VMEM)
    scratch = [
        pltpu.VMEM((dps - 1, rows, depth), BF16),
        pltpu.VMEM((2, half, depth // CORES), BF16),
        pltpu.VMEM((depth, 128), F32),
        pltpu.VMEM((depth, kvw), BF16),
        pltpu.VMEM((CORES, halves, kvw // halves, kvw), BF16),
        pltpu.VMEM((CORES, kvw, kvw), BF16),
        pltpu.VMEM((rows, kvw), F32),
        pltpu.VMEM((rows, 128), F32),
        pltpu.VMEM((rows, kvw), F32),
        pltpu.VMEM((half, kvw), F32),
        pltpu.VMEM((rows, kvw), BF16),
        pltpu.VMEM((2, half, kvw), BF16),
        pltpu.VMEM((2, rows, kvw), BF16),
        pltpu.VMEM((CORES, 2, half, kvw), BF16),
        pltpu.VMEM((CORES, half, kvw), F32),
        pltpu.VMEM((half, kvw), BF16),
        pltpu.VMEM((half, kvw), BF16),
        pltpu.VMEM((CORES, half, kvw), F32),
        pltpu.VMEM((CORES, half, kvw), F32),
        pltpu.VMEM((CORES, half, 128), F32),
        pltpu.VMEM((CORES, half, kvw), BF16),
        pltpu.VMEM((seqs * rows, kvw), BF16),
        pltpu.VMEM((rows, 128), F32),
        pltpu.VMEM((8, rows), F32),
        pltpu.VMEM((seqs - 1, 8, rows), F32),
        pltpu.VMEM((half, kvw), BF16),
        pltpu.VMEM((half, kvw), BF16),
        pltpu.VMEM((CORES, half, kvw), BF16),
        pltpu.VMEM((RING * rows, kvw), BF16),
        pltpu.VMEM((seqs - 1, rows, window), BF16),
        pltpu.VMEM((seqs * rows, window), BF16),
        pltpu.VMEM((384, seqs * rows), BF16),
        pltpu.VMEM(block, BF16),
        pltpu.VMEM((2, block[0] // 2, block[1]), BF16),
        pltpu.VMEM((2,) + block, BF16),
        pltpu.VMEM((2,) + block, BF16),
        pltpu.VMEM((2, 128, RING * rows), BF16),
        pltpu.VMEM((2, kvw // seqs, kvw), F32),
        pltpu.VMEM((2 * dps - 1,) + out_block, BF16),
        pltpu.VMEM((2 * dps - 1,) + out_block, BF16),
        dma((2, 2)),
        dma((2, 4)),
        dma((2, 3)),
        dma((2, seqs)),
        dma((2, dps - 1)),
        dma((2,)),
        dma((2, 2)),
        dma((2, CORES, 2, CORES)),
        dma((2, 2, PARTS)),
        dma((2, 3)),
        dma((2, 9)),
        dma((2, seqs - 1)),
        dma((2, 9)),
        dma((2, seqs - 1)),
        dma((2, 9)),
        dma((2, 4)),
        dma((2, 2 * dps - 1)),
    ]
    input_cov, output_cov = pl.pallas_call(
        functools.partial(kernel, token_count),
        out_shape=(
            jax.ShapeDtypeStruct(block, F32),
            jax.ShapeDtypeStruct(out_block, F32),
        ),
        in_specs=[vmem] * 4,
        out_specs=(vmem, vmem),
        scratch_shapes=scratch,
        compiler_params=pltpu.CompilerParams(
            collective_id=0, has_side_effects=True, vmem_limit_bytes=56 * 1024 * 1024
        ),
    )(
        hidden_in.reshape(rows, width),
        out_grad.reshape(rows, window),
        value_weight.reshape(depth, kvw),
        norm_gain,
    )
    return (input_cov[None], output_cov.T[None])


def solution(mesh):
    return jax.shard_map(
        on_device,
        mesh=mesh,
        in_specs=(
            P(None, "dp", "seq", None),
            P(None, "dp", "seq", None),
            P("section", "dp", None),
            P("section", None),
        ),
        out_specs=(P("section", "seq", "dp"), P("section", "dp", "seq")),
        check_vma=False,
    )
```

```python
import jax
import jax.numpy as jnp
from jax import lax
from jax.experimental import pallas as pl
from jax.experimental.pallas import tpu as pltpu
from jax.sharding import PartitionSpec as P

HEAD = 128
GROUP = 5
CORES = 2
RING = 4
PARTS = 4
AHEAD = 4
EARLY = 4

epsilon = 1e-06

MESH = pl.DeviceIdType.MESH
F32 = jnp.float32
BF16 = jnp.bfloat16


def column(row):
    return jnp.transpose(jnp.broadcast_to(row, (128, 128)))


def kernel(
    hidden_ref,
    grad_ref,
    weight_ref,
    gain_ref,
    in_cov_ref,
    cov_in,
    out_cov_ref,
    out_recv,
    crossed,
    relayed,
    gain_col,
    scaled,
    cmat,
    cmat_t,
    mean5,
    spare,
    own_out,
    own_in,
    far_out,
    far_in,
    near_out,
    near_in,
    base,
    chain_in,
    chain_out,
    centred,
    product,
    inverse,
    states,
    state,
    inverse_all,
    inverse_row,
    inverse_in,
    grad_in,
    grad_out,
    dvalues,
    grads,
    hidden_in,
    rows_all,
    left_t,
    cov_far,
    cov_relay,
    cov_near,
    left_g,
    turned,
    out_send,
    cross_sem,
    relay_sem,
    pair_sem,
    share_sem,
    cmat_sem,
    fold_sem,
    own_sem,
    far_sem,
    near_sem,
    chain_sem,
    lend_sem,
    hidden_sem,
    hidden_share,
    state_sem,
    state_first,
    inverse_sem,
    grads_sem,
    grads_first,
    cov_sem,
    out_sem,
):
    section = lax.axis_index("section")
    seq = lax.axis_index("seq")
    dp = lax.axis_index("dp")
    sections = lax.axis_size("section")
    seqs = lax.axis_size("seq")
    dps = lax.axis_size("dp")
    rows, width = hidden_ref.shape
    window = grad_ref.shape[1]
    depth, kvw = weight_ref.shape
    heads = kvw // HEAD
    chip = section // CORES
    core = section % CORES
    sibling = chip * CORES + (1 - core)
    has_left = chip > 0
    has_right = chip < sections // CORES - 1
    x = seq % RING
    z_low = seq // RING
    x_next = z_low * RING + (x + 1) % RING
    x_last = z_low * RING + (x + RING - 1) % RING
    z_pair = (1 - z_low) * RING + x
    dp_next = (dp + 1) % dps
    dp_last = (dp + dps - 1) % dps
    half = rows // CORES
    step = half // PARTS

    sent = []

    def remote(src, dst, sem, *index, **device):
        return pltpu.make_async_remote_copy(
            src_ref=src,
            dst_ref=dst,
            send_sem=sem.at[(0,) + index],
            recv_sem=sem.at[(1,) + index],
            device_id=device,
            device_id_type=MESH,
        )

    def start(copy):
        copy.start()
        sent.append(copy)

    barrier = pltpu.get_barrier_semaphore()

    def greet(**device):
        pl.semaphore_signal(barrier, inc=1, device_id=device, device_id_type=MESH)

    for k in range(1, dps):
        greet(dp=(dp + k) % dps)
        greet(dp=(dp + k) % dps, seq=z_pair)
    for j in range(1, seqs):
        greet(seq=seq ^ j)
    greet(section=sibling)
    greet(section=sibling, dp=dp_next)
    greet(section=sibling, dp=dp_last)
    for other in (z_pair, x_next, x_last):
        greet(section=sibling, seq=other)

    @pl.when(has_left)
    def _():
        greet(section=section - CORES)

    @pl.when(has_right)
    def _():
        greet(section=section + CORES)

    pl.semaphore_wait(
        barrier,
        2 * (dps - 1) + seqs - 1 + 6 + has_left.astype(jnp.int32) + has_right.astype(jnp.int32),
    )

    piece = depth // CORES
    my_piece = pl.ds(pl.multiple_of(core * piece, 128), piece)
    side = chip % 2
    pair = section + CORES - 2 * CORES * side
    quarter = half // 2
    my_half = pl.ds(pl.multiple_of(side * half, 16), half)

    def columns_of(other):
        return pl.ds(pl.multiple_of(other * depth + core * piece, 128), piece)

    def cross(k):
        other = dp_next if k == 0 else dp_last
        return remote(
            hidden_ref.at[my_half, columns_of(other)],
            crossed.at[2 * k, my_half, my_piece],
            cross_sem,
            k,
            dp=other,
        )

    far_columns = columns_of((dp + 2) % dps)

    def my_quarter(k):
        return pl.ds(pl.multiple_of(side * half + k * quarter, 16), quarter)

    def far_first(k):
        return remote(
            hidden_ref.at[my_quarter(k), far_columns],
            relayed.at[k],
            relay_sem,
            k,
            dp=dp_next if k == 0 else dp_last,
        )

    def far_second(k):
        return remote(
            relayed.at[k],
            crossed.at[1, my_quarter(k), my_piece],
            relay_sem,
            2 + k,
            dp=dp_next if k == 0 else dp_last,
        )

    def share_pair(slot):
        where = crossed.at[slot, my_half, my_piece]
        return remote(where, where, pair_sem, slot, section=pair)

    def share(slot):
        return remote(
            crossed.at[slot, :, my_piece],
            crossed.at[slot, :, my_piece],
            share_sem,
            slot,
            section=sibling,
        )

    start(far_first(0))
    start(far_first(1))
    start(cross(0))
    start(cross(1))

    first = pl.multiple_of(dp * depth, 128)

    @pl.loop(0, depth // HEAD)
    def _(block):
        where = pl.ds(pl.multiple_of(block * HEAD, HEAD), HEAD)
        gain_here = column(gain_ref[:, pl.ds(pl.multiple_of(first + block * HEAD, HEAD), HEAD)])
        gain_col[where, :] = gain_here
        for c in range(kvw // 128):
            lanes = pl.ds(c * 128, 128)
            scaled[where, lanes] = (weight_ref[where, lanes].astype(F32) * gain_here).astype(BF16)

    halves = window // depth
    fold_rows = kvw // halves
    chunk = fold_rows // seqs
    fold_here = pl.ds(pl.multiple_of(seq * chunk, 16), chunk)

    def give_fold(k, part):
        where = cmat.at[core, part, fold_here]
        return pltpu.make_async_remote_copy(
            src_ref=where,
            dst_ref=where,
            send_sem=fold_sem.at[0, k - 1],
            recv_sem=fold_sem.at[1, part],
            device_id={"dp": (dp + k) % dps},
            device_id_type=MESH,
        )

    def give_cmat(j):
        where = cmat.at[core, :, fold_here]
        return remote(where, where, cmat_sem, j - 1, seq=seq ^ j)

    def share_cmat():
        return remote(cmat.at[core], cmat.at[core], cmat_sem, seqs - 1, section=sibling)

    @pl.when(dp < halves)
    def _():
        per_head = HEAD // chunk
        row = (seq // per_head) * (GROUP * HEAD) + (seq % per_head) * chunk
        for c in range(kvw // 128):
            lanes = pl.ds(c * 128, 128)
            total = None
            for q in range(GROUP):
                where = pl.ds(pl.multiple_of(row + q * HEAD, 16), chunk)
                term = weight_ref[where, lanes].astype(F32) * gain_col[where, :]
                total = term if total is None else total + term
            cmat[core, dp, fold_here, lanes] = total.astype(BF16)
        for k in range(1, dps):
            give_fold(k, dp).start()

    def give_own():
        return remote(
            own_out.at[pl.ds(pl.multiple_of((1 - core) * half, 16), half)],
            own_in,
            own_sem,
            section=sibling,
        )

    own_out[...] = jnp.dot(
        hidden_ref[:, pl.ds(first, depth)], scaled[...], preferred_element_type=F32
    )
    start(give_own())

    for part in range(halves):

        @pl.when(dp != part)
        def _():
            give_fold(1, part).wait_recv()

    for j in range(1, seqs):
        start(give_cmat(j))

    def ring(sem, view):
        front, back = (0, half), (half, half)
        full = (0, rows)
        plan = (
            (0, 4, full, z_pair),
            (0, 1, full, x_next),
            (0, 2, full, x_last),
            (4, 5, full, x_next),
            (4, 6, full, x_last),
            (1, 3, front, x_next),
            (2, 3, back, x_last),
            (5, 7, front, x_next),
            (6, 7, back, x_last),
        )

        def copy(i):
            src, dst, part, device = plan[i]
            return remote(view(src, *part), view(dst, *part), sem, i, seq=device)

        return copy

    wide = window // CORES
    my_wide = pl.ds(pl.multiple_of(core * wide, 128), wide)

    def hidden_view(slot, low, count):
        if slot == 0:
            return hidden_ref.at[pl.ds(low, count), my_wide]
        return hidden_in.at[slot - 1, pl.ds(low, count), my_wide]

    def share_hidden(slot):
        where = hidden_in.at[slot - 1, :, my_wide]
        return remote(where, where, hidden_share, slot - 1, section=sibling)

    give_hidden = ring(hidden_sem, hidden_view)
    give_state = ring(state_sem, lambda slot, low, count: state.at[pl.ds(slot * rows + low, count)])
    give_grads = ring(grads_sem, lambda slot, low, count: grads.at[pl.ds(slot * rows + low, count)])

    def give_inverse(slot):
        z_there = z_low if slot < RING else 1 - z_low
        x_there = (x + (0, 1, 3, 2)[slot % RING]) % RING
        return remote(
            inverse_row,
            inverse_in.at[slot - 1],
            inverse_sem,
            slot - 1,
            seq=z_there * RING + x_there,
        )

    start(give_hidden(1))
    start(give_hidden(2))

    for k in range(2):
        far_first(k).wait_recv()
        start(far_second(k))

    fixed = jnp.zeros((rows, HEAD), F32)
    for k in range(heads):
        parts = [
            hidden_ref[:, pl.ds((k * GROUP + q) * HEAD, HEAD)].astype(F32) for q in range(GROUP)
        ]
        mean = (parts[0] + parts[1] + parts[2] + parts[3] + parts[4]) * (1.0 / GROUP)
        mean5[:, pl.ds(k * HEAD, HEAD)] = mean
        for part in parts:
            fixed = fixed + (part - mean) * (part - mean)
    for b in range(window // HEAD, width // HEAD):
        part = hidden_ref[:, pl.ds(b * HEAD, HEAD)].astype(F32)
        fixed = fixed + part * part
    spare[...] = jnp.broadcast_to(jnp.sum(fixed, axis=1, keepdims=True), (rows, 128))

    my_rows = pl.ds(pl.multiple_of(core * half, 16), half)

    @pl.when(chip == 0)
    def _():
        chain_in[...] = jnp.zeros((half, kvw), BF16)

    @pl.when(jnp.logical_not(has_right))
    def _():
        for k in range(heads):
            total = grad_ref[my_rows, pl.ds(k * GROUP * HEAD, HEAD)].astype(F32)
            for q in range(1, GROUP):
                total = total + grad_ref[my_rows, pl.ds((k * GROUP + q) * HEAD, HEAD)].astype(F32)
            grad_in[:, pl.ds(k * HEAD, HEAD)] = total.astype(BF16)

    cross(0).wait_recv()
    start(share_pair(0))
    cross(1).wait_recv()
    start(share_pair(2))
    for k in range(2):
        far_second(k).wait_recv()
    start(share_pair(1))
    for slot in (0, 2, 1):
        share_pair(slot).wait_recv()
        start(share(slot))

    def partial_rows(slot):
        share(slot).wait_recv()
        return jnp.dot(crossed[slot], scaled[...], preferred_element_type=F32)

    def give_far(k):
        return remote(
            far_out.at[pl.ds(k * half, half)],
            far_in.at[k],
            far_sem,
            k,
            dp=dp_next if k == 0 else dp_last,
        )

    def give_near(way, other_core):
        return remote(
            near_out.at[way, pl.ds(other_core * half, half)],
            near_in.at[core, way],
            near_sem,
            core,
            way,
            other_core,
            dp=dp_next if way == 0 else dp_last,
            section=chip * CORES + other_core,
        )

    def near_arrived(layer, way):
        where = near_in.at[layer, way]
        pltpu.make_async_remote_copy(
            src_ref=where,
            dst_ref=where,
            send_sem=near_sem.at[0, layer, way, core],
            recv_sem=near_sem.at[1, layer, way, core],
            device_id={"dp": dp_next},
            device_id_type=MESH,
        ).wait_recv()

    near_last = partial_rows(0)
    near_out[1, pl.ds(0, half), :] = near_last[:half].astype(BF16)
    start(give_near(1, 0))
    near_next = partial_rows(2)
    near_out[0, pl.ds(half, half), :] = near_next[half:].astype(BF16)
    start(give_near(0, 1))
    far_out[...] = partial_rows(1).astype(BF16)
    start(give_far(0))
    start(give_far(1))

    for j in range(1, seqs):
        give_cmat(j).wait_recv()
    start(share_cmat())

    give_far(0).wait_recv()
    near_out[0, pl.ds(0, half), :] = (near_next[:half] + far_in[0].astype(F32)).astype(BF16)
    start(give_near(0, 0))
    give_far(1).wait_recv()
    near_out[1, pl.ds(half, half), :] = (near_last[half:] + far_in[1].astype(F32)).astype(BF16)
    start(give_near(1, 1))

    start(give_hidden(0))
    give_hidden(1).wait_recv()
    start(give_hidden(5))
    start(share_hidden(1))
    give_hidden(2).wait_recv()
    start(give_hidden(6))
    start(share_hidden(2))

    share_cmat().wait_recv()
    for layer in range(CORES):
        cmat_t[layer] = jnp.transpose(cmat[layer].reshape(kvw, kvw))

    give_own().wait_recv()
    for layer in range(CORES):
        near_arrived(layer, 0)
        near_arrived(layer, 1)
        own = jnp.where(core == layer, own_out[my_rows, :], own_in[...])
        base[layer] = own + (near_in[layer, 0].astype(F32) + near_in[layer, 1].astype(F32))

    def pass_hidden():
        give_hidden(0).wait_recv()
        give_hidden(3).start()
        give_hidden(4).start()
        share_hidden(4).start()

    @pl.when(chip >= AHEAD)
    def _():
        pass_hidden()

    def send_forward(i):
        where = pl.ds(i * step, step)
        return remote(
            chain_out.at[where], chain_in.at[where], chain_sem, 0, i, section=section + CORES
        )

    def send_backward(i):
        where = pl.ds(i * step, step)
        return remote(
            grad_out.at[where], grad_in.at[where], chain_sem, 1, i, section=section - CORES
        )

    for i in range(PARTS):
        where = pl.ds(i * step, step)
        here = pl.ds(pl.multiple_of(core * half + i * step, 16), step)

        @pl.when(has_left)
        def _():
            send_forward(i).wait_recv()

        s = chain_in[where, :]
        s32 = s.astype(F32)
        for layer in range(CORES):
            c32 = s32 + mean5[here, :]
            squares = spare[here, 0:1] + GROUP * jnp.sum(c32 * c32, axis=1, keepdims=True)
            inv = lax.rsqrt(squares * (1.0 / width) + epsilon)
            prod = (
                jnp.dot(s, cmat[layer].reshape(kvw, kvw), preferred_element_type=F32)
                + base[layer, where, :]
            )
            states[layer, where, :] = s
            centred[layer, where, :] = c32
            product[layer, where, :] = prod
            inverse[layer, where, :] = jnp.broadcast_to(inv, (step, 128))
            s32 = s32 + inv * prod
            s = s32.astype(BF16)
        chain_out[where, :] = s

        @pl.when(has_right)
        def _():
            send_forward(i).start()

    def lend_state():
        return remote(states.at[1 - core], state.at[my_rows], lend_sem, 0, section=sibling)

    def lend_inverse():
        return remote(inverse.at[1 - core], inverse_all.at[my_rows], lend_sem, 1, section=sibling)

    def lend_grads():
        return remote(dvalues.at[1 - core], grads.at[my_rows], lend_sem, 2, section=sibling)

    def first_step(i, layer, source, target, sem):
        slot = (4, 1, 2)[i]
        where = pl.ds(pl.multiple_of(slot * rows + core * half, 16), half)
        return pltpu.make_async_remote_copy(
            src_ref=source.at[layer],
            dst_ref=target.at[where],
            send_sem=sem.at[0, i, layer],
            recv_sem=sem.at[1, i, core],
            device_id={"section": chip * CORES + layer, "seq": (z_pair, x_next, x_last)[i]},
            device_id_type=MESH,
        )

    def first_arrived(i, source, target, sem):
        for other in range(CORES):
            where = target.at[pl.ds((4, 1, 2)[i] * rows + other * half, half)]
            pltpu.make_async_remote_copy(
                src_ref=where,
                dst_ref=where,
                send_sem=sem.at[0, i, other],
                recv_sem=sem.at[1, i, other],
                device_id={"seq": x_next},
                device_id_type=MESH,
            ).wait_recv()

    first_state = (states, state, state_first)
    first_grads = (dvalues, grads, grads_first)

    for i in (1, 2, 0):
        for layer in range(CORES):
            start(first_step(i, layer, *first_state))
    start(lend_inverse())
    start(lend_state())
    state[my_rows, :] = states[core]
    inverse_all[my_rows, :] = inverse[core]
    lend_inverse().wait_recv()
    inverse_row[...] = jnp.transpose(inverse_all[...])[0:8, :]
    for slot in range(1, seqs):
        start(give_inverse(slot))
    lend_state().wait_recv()

    @pl.when(chip < AHEAD)
    def _():
        pass_hidden()

    def backward():
        for i in range(PARTS):
            where = pl.ds(i * step, step)

            @pl.when(has_right)
            def _():
                send_backward(i).wait_recv()

            def turn(g, g32, layer):
                other = jnp.dot(g, cmat_t[layer], preferred_element_type=F32)
                inner = jnp.sum(g32 * product[layer, where, :], axis=1, keepdims=True)
                inv = inverse[layer, where, 0:1]
                factor = inv * inv * inner * (GROUP / width)
                return g32 + inv * (other - centred[layer, where, :] * factor)

            g = grad_in[where, :]
            dvalues[1, where, :] = g
            g32 = turn(g, g.astype(F32), 1)
            g = g32.astype(BF16)
            dvalues[0, where, :] = g

            @pl.when(has_left)
            def _():
                grad_out[where, :] = turn(g, g.astype(F32), 0).astype(BF16)
                send_backward(i).start()

        for i in (1, 2):
            for layer in range(CORES):
                first_step(i, layer, *first_grads).start()
        lend_grads().start()
        grads[my_rows, :] = dvalues[core]

    begin = pl.multiple_of((seq // 2) * (GROUP * HEAD) + (seq % 2) * 256, 128)
    odd = seq % 2
    block_rows, block_cols = in_cov_ref.shape
    cov_half = block_rows // 2

    def fill(slot, read_hidden, inv):
        here = pl.ds(slot * rows, rows)
        for k in range(heads):
            s32 = state[here, pl.ds(k * HEAD, HEAD)].astype(F32)
            for q in range(GROUP):
                lanes = pl.ds((k * GROUP + q) * HEAD, HEAD)
                rows_all[here, lanes] = (read_hidden(lanes).astype(F32) + s32).astype(BF16)
        factor = inv * inv
        for c in range(3):
            lanes = pl.ds(pl.multiple_of(begin + c * 128, 128), 128)
            part = rows_all[here, lanes].astype(F32) * factor * gain_ref[:, lanes]
            left_t[pl.ds(c * 128, 128), here] = jnp.transpose(part).astype(BF16)

    def give_cov_far(k):
        return remote(
            cov_far.at[pl.ds(k * cov_half, cov_half)],
            cov_relay.at[k],
            cov_sem,
            k,
            dp=dp_next if k == 0 else dp_last,
        )

    def give_cov(k):
        return remote(
            cov_near.at[k], cov_in.at[k], cov_sem, 2 + k, dp=dp_next if k == 0 else dp_last
        )

    def input_cov():
        def take(slot):
            share_hidden(slot).wait_recv()
            give_inverse(slot).wait_recv()
            fill(
                slot,
                lambda lanes: hidden_in[slot - 1, :, lanes],
                column(inverse_in[slot - 1, 0:1, :]),
            )

        first_arrived(1, *first_state)
        give_state(5).start()
        first_arrived(2, *first_state)
        give_state(6).start()
        first_arrived(0, *first_state)
        give_state(3).start()
        give_state(4).start()
        give_hidden(3).wait_recv()
        give_hidden(7).start()
        share_hidden(5).start()
        give_hidden(4).wait_recv()
        give_hidden(8).start()
        share_hidden(6).start()
        give_hidden(5).wait_recv()
        give_hidden(6).wait_recv()
        share_hidden(3).start()
        fill(0, lambda lanes: hidden_ref[:, lanes], inverse_all[...])
        take(1)
        give_state(3).wait_recv()
        give_state(7).start()
        give_state(4).wait_recv()
        give_state(8).start()
        take(2)
        take(4)
        give_hidden(7).wait_recv()
        give_hidden(8).wait_recv()
        share_hidden(7).start()
        give_state(5).wait_recv()
        give_state(6).wait_recv()
        take(3)
        take(5)
        take(6)
        give_state(7).wait_recv()
        give_state(8).wait_recv()
        take(7)

        def block(other):
            lanes = pl.ds(pl.multiple_of(other * block_cols, 128), block_cols)
            part = jnp.dot(left_t[...], rows_all[:, lanes], preferred_element_type=F32)
            part = part * gain_ref[:, lanes]
            return jnp.where(odd == 0, part[:block_rows], part[64 : 64 + block_rows])

        cov_far[...] = block((dp + 2) % dps).astype(BF16)
        give_cov_far(0).start()
        give_cov_far(1).start()
        in_cov_ref[...] = block(dp)
        part = block(dp_next)
        cov_near[0, pl.ds(cov_half, cov_half), :] = part[cov_half:].astype(BF16)
        give_cov_far(0).wait_recv()
        cov_near[0, pl.ds(0, cov_half), :] = (
            part[:cov_half] + cov_relay[0].astype(F32)
        ).astype(BF16)
        give_cov(0).start()
        part = block(dp_last)
        cov_near[1, pl.ds(0, cov_half), :] = part[:cov_half].astype(BF16)
        give_cov_far(1).wait_recv()
        cov_near[1, pl.ds(cov_half, cov_half), :] = (
            part[cov_half:] + cov_relay[1].astype(F32)
        ).astype(BF16)
        give_cov(1).start()

    early = chip <= EARLY

    @pl.loop(0, 2)
    def _(phase):
        @pl.when((phase == 0) == early)
        def _():
            input_cov()

        @pl.when((phase == 0) != early)
        def _():
            backward()

    first_arrived(1, *first_grads)
    start(give_grads(5))
    first_arrived(2, *first_grads)
    start(give_grads(6))
    lend_grads().wait_recv()
    out_rows = out_cov_ref.shape[0]
    for z in range(2):
        lanes = pl.ds(pl.multiple_of(z * (kvw // 2) + (x // 2) * 128, 128), 128)
        for slot in range(3):
            here = pl.ds(slot * rows, rows)
            left_g[z, :, here] = jnp.transpose(grads[here, lanes].astype(F32)).astype(BF16)
    give_grads(5).wait_recv()
    give_grads(6).wait_recv()
    for z in range(2):
        lanes = pl.ds(pl.multiple_of(z * (kvw // 2) + (x // 2) * 128, 128), 128)
        here = pl.ds(3 * rows, rows)
        left_g[z, :, here] = jnp.transpose(grads[here, lanes].astype(F32)).astype(BF16)
        mine = pl.ds(pl.multiple_of((x % 2) * out_rows, 16), out_rows)
        turned[z] = jnp.dot(
            left_g[z, mine, :], grads[pl.ds(0, RING * rows), :], preferred_element_type=F32
        )

    def block_of(k):
        z = z_low if k % 2 == 0 else 1 - z_low
        lanes = pl.ds(pl.multiple_of(((dp + k // 2) % dps) * HEAD, 128), HEAD)
        return turned[z, :, lanes]

    def give_out(k):
        return remote(
            out_send.at[k - 1],
            out_recv.at[k - 1],
            out_sem,
            k - 1,
            dp=(dp + k // 2) % dps,
            seq=seq if k % 2 == 0 else z_pair,
        )

    for k in range(1, 2 * dps):
        out_send[k - 1] = block_of(k).astype(BF16)
        start(give_out(k))

    out_cov_ref[...] = block_of(0)
    for k in range(2):
        give_cov(k).wait_recv()
    for k in range(1, 2 * dps):
        give_out(k).wait_recv()

    for copy in sent:
        copy.wait_send()
    for slot in (3, 5, 6, 7):
        share_hidden(slot).wait_send()
    for i in (7, 8):
        give_hidden(i).wait_send()
    for i in range(3, 9):
        give_state(i).wait_send()
    for i in (1, 2):
        for layer in range(CORES):
            first_step(i, layer, *first_grads).wait_send()
    lend_grads().wait_send()
    for i in (3, 4):
        give_hidden(i).wait_send()
    share_hidden(4).wait_send()
    for k in range(2):
        give_cov_far(k).wait_send()
        give_cov(k).wait_send()

    @pl.when(dp < halves)
    def _():
        for k in range(1, dps):
            give_fold(k, dp).wait_send()

    @pl.when(has_right)
    def _():
        for i in range(PARTS):
            send_forward(i).wait_send()

    @pl.when(has_left)
    def _():
        for i in range(PARTS):
            send_backward(i).wait_send()


def on_device(hidden_in, out_grad, value_weight, norm_gain):
    seqs = lax.axis_size("seq")
    dps = lax.axis_size("dp")
    rows, width = hidden_in.shape[2:]
    window = out_grad.shape[3]
    depth, kvw = value_weight.shape[1:]
    token_count = rows * seqs * dps
    half = rows // CORES
    block = (window // seqs, window // dps)
    out_block = (kvw // seqs, kvw // dps)
    halves = window // depth
    dma = pltpu.SemaphoreType.DMA
    vmem = pl.BlockSpec(memory_space=pltpu.VMEM)
    scratch = [
        pltpu.VMEM((dps - 1, rows, depth), BF16),
        pltpu.VMEM((2, half // 2, depth // CORES), BF16),
        pltpu.VMEM((depth, 128), F32),
        pltpu.VMEM((depth, kvw), BF16),
        pltpu.VMEM((CORES, halves, kvw // halves, kvw), BF16),
        pltpu.VMEM((CORES, kvw, kvw), BF16),
        pltpu.VMEM((rows, kvw), F32),
        pltpu.VMEM((rows, 128), F32),
        pltpu.VMEM((rows, kvw), F32),
        pltpu.VMEM((half, kvw), F32),
        pltpu.VMEM((rows, kvw), BF16),
        pltpu.VMEM((2, half, kvw), BF16),
        pltpu.VMEM((2, rows, kvw), BF16),
        pltpu.VMEM((CORES, 2, half, kvw), BF16),
        pltpu.VMEM((CORES, half, kvw), F32),
        pltpu.VMEM((half, kvw), BF16),
        pltpu.VMEM((half, kvw), BF16),
        pltpu.VMEM((CORES, half, kvw), F32),
        pltpu.VMEM((CORES, half, kvw), F32),
        pltpu.VMEM((CORES, half, 128), F32),
        pltpu.VMEM((CORES, half, kvw), BF16),
        pltpu.VMEM((seqs * rows, kvw), BF16),
        pltpu.VMEM((rows, 128), F32),
        pltpu.VMEM((8, rows), F32),
        pltpu.VMEM((seqs - 1, 8, rows), F32),
        pltpu.VMEM((half, kvw), BF16),
        pltpu.VMEM((half, kvw), BF16),
        pltpu.VMEM((CORES, half, kvw), BF16),
        pltpu.VMEM((RING * rows, kvw), BF16),
        pltpu.VMEM((seqs - 1, rows, window), BF16),
        pltpu.VMEM((seqs * rows, window), BF16),
        pltpu.VMEM((384, seqs * rows), BF16),
        pltpu.VMEM(block, BF16),
        pltpu.VMEM((2, block[0] // 2, block[1]), BF16),
        pltpu.VMEM((2,) + block, BF16),
        pltpu.VMEM((2, 128, RING * rows), BF16),
        pltpu.VMEM((2, kvw // seqs, kvw), F32),
        pltpu.VMEM((2 * dps - 1,) + out_block, BF16),
        dma((2, 2)),
        dma((2, 4)),
        dma((2, 3)),
        dma((2, 3)),
        dma((2, seqs)),
        dma((2, dps - 1)),
        dma((2,)),
        dma((2, 2)),
        dma((2, CORES, 2, CORES)),
        dma((2, 2, PARTS)),
        dma((2, 3)),
        dma((2, 9)),
        dma((2, seqs - 1)),
        dma((2, 9)),
        dma((2, 3, CORES)),
        dma((2, seqs - 1)),
        dma((2, 9)),
        dma((2, 3, CORES)),
        dma((2, 4)),
        dma((2, 2 * dps - 1)),
    ]
    input_own, input_parts, output_own, output_parts = pl.pallas_call(
        kernel,
        out_shape=(
            jax.ShapeDtypeStruct(block, F32),
            jax.ShapeDtypeStruct((2,) + block, BF16),
            jax.ShapeDtypeStruct(out_block, F32),
            jax.ShapeDtypeStruct((2 * dps - 1,) + out_block, BF16),
        ),
        in_specs=[vmem] * 4,
        out_specs=(vmem,) * 4,
        scratch_shapes=scratch,
        compiler_params=pltpu.CompilerParams(
            collective_id=0, has_side_effects=True, vmem_limit_bytes=56 * 1024 * 1024
        ),
    )(
        hidden_in.reshape(rows, width),
        out_grad.reshape(rows, window),
        value_weight.reshape(depth, kvw),
        norm_gain,
    )
    input_cov = input_own + (input_parts[0].astype(F32) + input_parts[1].astype(F32))
    output_cov = output_own + jnp.sum(output_parts.astype(F32), axis=0)
    return (input_cov[None] / token_count, output_cov.T[None] / token_count)


def solution(mesh):
    return jax.shard_map(
        on_device,
        mesh=mesh,
        in_specs=(
            P(None, "dp", "seq", None),
            P(None, "dp", "seq", None),
            P("section", "dp", None),
            P("section", None),
        ),
        out_specs=(P("section", "seq", "dp"), P("section", "dp", "seq")),
        check_vma=False,
    )
```

```python
import jax
import jax.numpy as jnp
from jax import lax
from jax.experimental import pallas as pl
from jax.experimental.pallas import tpu as pltpu
from jax.sharding import PartitionSpec as P

HEAD = 128
GROUP = 5
CORES = 2
RING = 4
PARTS = 4
AHEAD = 4
EARLY = 4

epsilon = 1e-06

MESH = pl.DeviceIdType.MESH
F32 = jnp.float32
BF16 = jnp.bfloat16


def column(row):
    return jnp.transpose(jnp.broadcast_to(row, (128, 128)))


def kernel(
    hidden_ref,
    grad_ref,
    weight_ref,
    gain_ref,
    in_cov_ref,
    cov_in,
    out_cov_ref,
    out_recv,
    crossed,
    relayed,
    gain_col,
    scaled,
    cmat,
    cmat_t,
    mean5,
    spare,
    own_out,
    own_in,
    far_out,
    far_in,
    near_out,
    near_in,
    base,
    chain_in,
    chain_out,
    centred,
    product,
    inverse,
    states,
    state,
    inverse_all,
    inverse_row,
    inverse_in,
    grad_in,
    grad_out,
    dvalues,
    grads,
    hidden_in,
    rows_all,
    left_t,
    cov_far,
    cov_relay,
    cov_near,
    left_g,
    turned,
    out_send,
    cross_sem,
    relay_sem,
    pair_sem,
    share_sem,
    cmat_sem,
    fold_sem,
    own_sem,
    far_sem,
    near_sem,
    chain_sem,
    lend_sem,
    hidden_sem,
    hidden_share,
    state_sem,
    state_first,
    inverse_sem,
    grads_sem,
    grads_first,
    cov_sem,
    out_sem,
):
    section = lax.axis_index("section")
    seq = lax.axis_index("seq")
    dp = lax.axis_index("dp")
    sections = lax.axis_size("section")
    seqs = lax.axis_size("seq")
    dps = lax.axis_size("dp")
    rows, width = hidden_ref.shape
    window = grad_ref.shape[1]
    depth, kvw = weight_ref.shape
    heads = kvw // HEAD
    chip = section // CORES
    core = section % CORES
    sibling = chip * CORES + (1 - core)
    has_left = chip > 0
    has_right = chip < sections // CORES - 1
    x = seq % RING
    z_low = seq // RING
    x_next = z_low * RING + (x + 1) % RING
    x_last = z_low * RING + (x + RING - 1) % RING
    z_pair = (1 - z_low) * RING + x
    dp_next = (dp + 1) % dps
    dp_last = (dp + dps - 1) % dps
    half = rows // CORES
    step = half // PARTS

    sent = []

    def remote(src, dst, sem, *index, **device):
        return pltpu.make_async_remote_copy(
            src_ref=src,
            dst_ref=dst,
            send_sem=sem.at[(0,) + index],
            recv_sem=sem.at[(1,) + index],
            device_id=device,
            device_id_type=MESH,
        )

    def start(copy):
        copy.start()
        sent.append(copy)

    barrier = pltpu.get_barrier_semaphore()

    def greet(**device):
        pl.semaphore_signal(barrier, inc=1, device_id=device, device_id_type=MESH)

    for k in range(1, dps):
        greet(dp=(dp + k) % dps)
        greet(dp=(dp + k) % dps, seq=z_pair)
    for j in range(1, seqs):
        greet(seq=seq ^ j)
    greet(section=sibling)
    greet(section=sibling, dp=dp_next)
    greet(section=sibling, dp=dp_last)
    for other in (z_pair, x_next, x_last):
        greet(section=sibling, seq=other)

    @pl.when(has_left)
    def _():
        greet(section=section - CORES)

    @pl.when(has_right)
    def _():
        greet(section=section + CORES)

    pl.semaphore_wait(
        barrier,
        2 * (dps - 1) + seqs - 1 + 6 + has_left.astype(jnp.int32) + has_right.astype(jnp.int32),
    )

    piece = depth // CORES
    my_piece = pl.ds(pl.multiple_of(core * piece, 128), piece)
    side = chip % 2
    pair = section + CORES - 2 * CORES * side
    quarter = half // 2
    my_half = pl.ds(pl.multiple_of(side * half, 16), half)

    def columns_of(other):
        return pl.ds(pl.multiple_of(other * depth + core * piece, 128), piece)

    def cross(k):
        other = dp_next if k == 0 else dp_last
        return remote(
            hidden_ref.at[my_half, columns_of(other)],
            crossed.at[2 * k, my_half, my_piece],
            cross_sem,
            k,
            dp=other,
        )

    far_columns = columns_of((dp + 2) % dps)

    def my_quarter(k):
        return pl.ds(pl.multiple_of(side * half + k * quarter, 16), quarter)

    def far_first(k):
        return remote(
            hidden_ref.at[my_quarter(k), far_columns],
            relayed.at[k],
            relay_sem,
            k,
            dp=dp_next if k == 0 else dp_last,
        )

    def far_second(k):
        return remote(
            relayed.at[k],
            crossed.at[1, my_quarter(k), my_piece],
            relay_sem,
            2 + k,
            dp=dp_next if k == 0 else dp_last,
        )

    def share_pair(slot):
        where = crossed.at[slot, my_half, my_piece]
        return remote(where, where, pair_sem, slot, section=pair)

    def share(slot):
        return remote(
            crossed.at[slot, :, my_piece],
            crossed.at[slot, :, my_piece],
            share_sem,
            slot,
            section=sibling,
        )

    start(far_first(0))
    start(far_first(1))
    start(cross(0))
    start(cross(1))

    first = pl.multiple_of(dp * depth, 128)

    @pl.loop(0, depth // HEAD)
    def _(block):
        where = pl.ds(pl.multiple_of(block * HEAD, HEAD), HEAD)
        gain_here = column(gain_ref[:, pl.ds(pl.multiple_of(first + block * HEAD, HEAD), HEAD)])
        gain_col[where, :] = gain_here

    halves = window // depth
    fold_rows = kvw // halves
    chunk = fold_rows // seqs
    fold_here = pl.ds(pl.multiple_of(seq * chunk, 16), chunk)

    def give_fold(k, part):
        where = cmat.at[core, part, fold_here]
        return pltpu.make_async_remote_copy(
            src_ref=where,
            dst_ref=where,
            send_sem=fold_sem.at[0, k - 1],
            recv_sem=fold_sem.at[1, part],
            device_id={"dp": (dp + k) % dps},
            device_id_type=MESH,
        )

    def share_cmat():
        return remote(cmat.at[core], cmat.at[core], cmat_sem, 9, section=sibling)

    @pl.when(dp < halves)
    def _():
        per_head = HEAD // chunk
        row = (seq // per_head) * (GROUP * HEAD) + (seq % per_head) * chunk
        for c in range(kvw // 128):
            lanes = pl.ds(c * 128, 128)
            total = None
            for q in range(GROUP):
                where = pl.ds(pl.multiple_of(row + q * HEAD, 16), chunk)
                term = weight_ref[where, lanes].astype(F32) * gain_col[where, :]
                total = term if total is None else total + term
            cmat[core, dp, fold_here, lanes] = total.astype(BF16)
        for k in range(1, dps):
            give_fold(k, dp).start()

    @pl.loop(0, depth // HEAD)
    def _(block):
        where = pl.ds(pl.multiple_of(block * HEAD, HEAD), HEAD)
        for c in range(kvw // 128):
            lanes = pl.ds(c * 128, 128)
            scaled[where, lanes] = (
                weight_ref[where, lanes].astype(F32) * gain_col[where, :]
            ).astype(BF16)

    def give_own():
        return remote(
            own_out.at[pl.ds(pl.multiple_of((1 - core) * half, 16), half)],
            own_in,
            own_sem,
            section=sibling,
        )

    own_out[...] = jnp.dot(
        hidden_ref[:, pl.ds(first, depth)], scaled[...], preferred_element_type=F32
    )
    start(give_own())

    def slot_seq(slot):
        z_there = z_low if slot < RING else 1 - z_low
        return z_there * RING + (x + (0, RING - 1, 1, 2)[slot % RING]) % RING

    def ring(sem, view, fixed=False):
        count = chunk if fixed else rows
        front, back = (0, count // 2), (count // 2, count // 2)
        full = (0, count)
        plan = (
            (0, 4, full, z_pair),
            (0, 1, full, x_next),
            (0, 2, full, x_last),
            (4, 5, full, x_next),
            (4, 6, full, x_last),
            (1, 3, front, x_next),
            (2, 3, back, x_last),
            (5, 7, front, x_next),
            (6, 7, back, x_last),
        )

        def copy(i):
            src, dst, part, device = plan[i]
            source = view(src, *part)
            return remote(source, source if fixed else view(dst, *part), sem, i, seq=device)

        return copy

    wide = window // CORES
    my_wide = pl.ds(pl.multiple_of(core * wide, 128), wide)

    def hidden_view(slot, low, count):
        if slot == 0:
            return hidden_ref.at[pl.ds(low, count), my_wide]
        return hidden_in.at[slot - 1, pl.ds(low, count), my_wide]

    def share_hidden(slot):
        where = hidden_in.at[slot - 1, :, my_wide]
        return remote(where, where, hidden_share, slot - 1, section=sibling)

    def cmat_view(slot, low, count):
        begin = slot_seq(slot) * chunk + low
        return cmat.at[core, :, pl.ds(pl.multiple_of(begin, 16), count)]

    give_cmat = ring(cmat_sem, cmat_view, True)
    give_hidden = ring(hidden_sem, hidden_view)
    give_state = ring(state_sem, lambda slot, low, count: state.at[pl.ds(slot * rows + low, count)])
    give_grads = ring(grads_sem, lambda slot, low, count: grads.at[pl.ds(slot * rows + low, count)])

    def give_inverse(slot):
        z_there = z_low if slot < RING else 1 - z_low
        x_there = (x + (0, 1, 3, 2)[slot % RING]) % RING
        return remote(
            inverse_row,
            inverse_in.at[slot - 1],
            inverse_sem,
            slot - 1,
            seq=z_there * RING + x_there,
        )

    for k in range(2):
        far_first(k).wait_recv()
        start(far_second(k))

    cross(0).wait_recv()
    start(share_pair(0))
    cross(1).wait_recv()
    start(share_pair(2))
    for part in range(halves):

        @pl.when(dp != part)
        def _():
            give_fold(1, part).wait_recv()

    for i in range(3):
        start(give_cmat(i))
    for k in range(2):
        far_second(k).wait_recv()
    start(share_pair(1))
    for slot in (0, 2):
        share_pair(slot).wait_recv()
        start(share(slot))
    for i, onward in ((0, (3, 4)), (1, (5,)), (2, (6,))):
        give_cmat(i).wait_recv()
        for j in onward:
            start(give_cmat(j))
    share_pair(1).wait_recv()
    start(share(1))

    def partial_rows(slot):
        share(slot).wait_recv()
        return jnp.dot(crossed[slot], scaled[...], preferred_element_type=F32)

    def give_far(k):
        return remote(
            far_out.at[pl.ds(k * half, half)],
            far_in.at[k],
            far_sem,
            k,
            dp=dp_next if k == 0 else dp_last,
        )

    def give_near(way, other_core):
        return remote(
            near_out.at[way, pl.ds(other_core * half, half)],
            near_in.at[core, way],
            near_sem,
            core,
            way,
            other_core,
            dp=dp_next if way == 0 else dp_last,
            section=chip * CORES + other_core,
        )

    def near_arrived(layer, way):
        where = near_in.at[layer, way]
        pltpu.make_async_remote_copy(
            src_ref=where,
            dst_ref=where,
            send_sem=near_sem.at[0, layer, way, core],
            recv_sem=near_sem.at[1, layer, way, core],
            device_id={"dp": dp_next},
            device_id_type=MESH,
        ).wait_recv()

    near_last = partial_rows(0)
    near_out[1, pl.ds(0, half), :] = near_last[:half].astype(BF16)
    start(give_near(1, 0))
    near_next = partial_rows(2)
    near_out[0, pl.ds(half, half), :] = near_next[half:].astype(BF16)
    start(give_near(0, 1))
    far_out[...] = partial_rows(1).astype(BF16)
    start(give_far(0))
    start(give_far(1))
    for i in (3, 4):
        give_cmat(i).wait_recv()
        start(give_cmat(i + 4))
    start(give_hidden(1))
    start(give_hidden(2))

    fixed = jnp.zeros((rows, HEAD), F32)
    for k in range(heads):
        parts = [
            hidden_ref[:, pl.ds((k * GROUP + q) * HEAD, HEAD)].astype(F32) for q in range(GROUP)
        ]
        mean = (parts[0] + parts[1] + parts[2] + parts[3] + parts[4]) * (1.0 / GROUP)
        mean5[:, pl.ds(k * HEAD, HEAD)] = mean
        for part in parts:
            fixed = fixed + (part - mean) * (part - mean)
    for b in range(window // HEAD, width // HEAD):
        part = hidden_ref[:, pl.ds(b * HEAD, HEAD)].astype(F32)
        fixed = fixed + part * part
    spare[...] = jnp.broadcast_to(jnp.sum(fixed, axis=1, keepdims=True), (rows, 128))

    my_rows = pl.ds(pl.multiple_of(core * half, 16), half)

    @pl.when(chip == 0)
    def _():
        chain_in[...] = jnp.zeros((half, kvw), BF16)

    @pl.when(jnp.logical_not(has_right))
    def _():
        for k in range(heads):
            total = grad_ref[my_rows, pl.ds(k * GROUP * HEAD, HEAD)].astype(F32)
            for q in range(1, GROUP):
                total = total + grad_ref[my_rows, pl.ds((k * GROUP + q) * HEAD, HEAD)].astype(F32)
            grad_in[:, pl.ds(k * HEAD, HEAD)] = total.astype(BF16)

    for i in range(5, 9):
        give_cmat(i).wait_recv()
    start(share_cmat())

    give_far(0).wait_recv()
    near_out[0, pl.ds(0, half), :] = (near_next[:half] + far_in[0].astype(F32)).astype(BF16)
    start(give_near(0, 0))
    give_far(1).wait_recv()
    near_out[1, pl.ds(half, half), :] = (near_last[half:] + far_in[1].astype(F32)).astype(BF16)
    start(give_near(1, 1))

    start(give_hidden(0))
    give_hidden(1).wait_recv()
    start(give_hidden(5))
    start(share_hidden(1))
    give_hidden(2).wait_recv()
    start(give_hidden(6))
    start(share_hidden(2))

    share_cmat().wait_recv()
    for layer in range(CORES):
        cmat_t[layer] = jnp.transpose(cmat[layer].reshape(kvw, kvw))

    give_own().wait_recv()
    for layer in range(CORES):
        near_arrived(layer, 0)
        near_arrived(layer, 1)
        own = jnp.where(core == layer, own_out[my_rows, :], own_in[...])
        base[layer] = own + (near_in[layer, 0].astype(F32) + near_in[layer, 1].astype(F32))

    def pass_hidden():
        give_hidden(0).wait_recv()
        give_hidden(3).start()
        give_hidden(4).start()
        share_hidden(4).start()

    @pl.when(chip >= AHEAD)
    def _():
        pass_hidden()

    def send_forward(i):
        where = pl.ds(i * step, step)
        return remote(
            chain_out.at[where], chain_in.at[where], chain_sem, 0, i, section=section + CORES
        )

    def send_backward(i):
        where = pl.ds(i * step, step)
        return remote(
            grad_out.at[where], grad_in.at[where], chain_sem, 1, i, section=section - CORES
        )

    for i in range(PARTS):
        where = pl.ds(i * step, step)
        here = pl.ds(pl.multiple_of(core * half + i * step, 16), step)

        @pl.when(has_left)
        def _():
            send_forward(i).wait_recv()

        s = chain_in[where, :]
        s32 = s.astype(F32)
        for layer in range(CORES):
            c32 = s32 + mean5[here, :]
            squares = spare[here, 0:1] + GROUP * jnp.sum(c32 * c32, axis=1, keepdims=True)
            inv = lax.rsqrt(squares * (1.0 / width) + epsilon)
            prod = (
                jnp.dot(s, cmat[layer].reshape(kvw, kvw), preferred_element_type=F32)
                + base[layer, where, :]
            )
            states[layer, where, :] = s
            centred[layer, where, :] = c32
            product[layer, where, :] = prod
            inverse[layer, where, :] = jnp.broadcast_to(inv, (step, 128))
            s32 = s32 + inv * prod
            s = s32.astype(BF16)
        chain_out[where, :] = s

        @pl.when(has_right)
        def _():
            send_forward(i).start()

    def lend_state():
        return remote(states.at[1 - core], state.at[my_rows], lend_sem, 0, section=sibling)

    def lend_inverse():
        return remote(inverse.at[1 - core], inverse_all.at[my_rows], lend_sem, 1, section=sibling)

    def lend_grads():
        return remote(dvalues.at[1 - core], grads.at[my_rows], lend_sem, 2, section=sibling)

    def first_step(i, layer, source, target, sem):
        slot = (4, 1, 2)[i]
        where = pl.ds(pl.multiple_of(slot * rows + core * half, 16), half)
        return pltpu.make_async_remote_copy(
            src_ref=source.at[layer],
            dst_ref=target.at[where],
            send_sem=sem.at[0, i, layer],
            recv_sem=sem.at[1, i, core],
            device_id={"section": chip * CORES + layer, "seq": (z_pair, x_next, x_last)[i]},
            device_id_type=MESH,
        )

    def first_arrived(i, source, target, sem):
        for other in range(CORES):
            where = target.at[pl.ds((4, 1, 2)[i] * rows + other * half, half)]
            pltpu.make_async_remote_copy(
                src_ref=where,
                dst_ref=where,
                send_sem=sem.at[0, i, other],
                recv_sem=sem.at[1, i, other],
                device_id={"seq": x_next},
                device_id_type=MESH,
            ).wait_recv()

    first_state = (states, state, state_first)
    first_grads = (dvalues, grads, grads_first)

    for i in (1, 2, 0):
        for layer in range(CORES):
            start(first_step(i, layer, *first_state))
    start(lend_inverse())
    start(lend_state())
    state[my_rows, :] = states[core]
    inverse_all[my_rows, :] = inverse[core]
    lend_inverse().wait_recv()
    inverse_row[...] = jnp.transpose(inverse_all[...])[0:8, :]
    for slot in range(1, seqs):
        start(give_inverse(slot))
    lend_state().wait_recv()

    @pl.when(chip < AHEAD)
    def _():
        pass_hidden()

    def backward():
        for i in range(PARTS):
            where = pl.ds(i * step, step)

            @pl.when(has_right)
            def _():
                send_backward(i).wait_recv()

            def turn(g, g32, layer):
                other = jnp.dot(g, cmat_t[layer], preferred_element_type=F32)
                inner = jnp.sum(g32 * product[layer, where, :], axis=1, keepdims=True)
                inv = inverse[layer, where, 0:1]
                factor = inv * inv * inner * (GROUP / width)
                return g32 + inv * (other - centred[layer, where, :] * factor)

            g = grad_in[where, :]
            dvalues[1, where, :] = g
            g32 = turn(g, g.astype(F32), 1)
            g = g32.astype(BF16)
            dvalues[0, where, :] = g

            @pl.when(has_left)
            def _():
                grad_out[where, :] = turn(g, g.astype(F32), 0).astype(BF16)
                send_backward(i).start()

        for i in (1, 2):
            for layer in range(CORES):
                first_step(i, layer, *first_grads).start()
        lend_grads().start()
        grads[my_rows, :] = dvalues[core]

    begin = pl.multiple_of((seq // 2) * (GROUP * HEAD) + (seq % 2) * 256, 128)
    odd = seq % 2
    block_rows, block_cols = in_cov_ref.shape
    cov_half = block_rows // 2

    def fill(slot, read_hidden, inv):
        here = pl.ds(slot * rows, rows)
        for k in range(heads):
            s32 = state[here, pl.ds(k * HEAD, HEAD)].astype(F32)
            for q in range(GROUP):
                lanes = pl.ds((k * GROUP + q) * HEAD, HEAD)
                rows_all[here, lanes] = (read_hidden(lanes).astype(F32) + s32).astype(BF16)
        factor = inv * inv
        for c in range(3):
            lanes = pl.ds(pl.multiple_of(begin + c * 128, 128), 128)
            part = rows_all[here, lanes].astype(F32) * factor * gain_ref[:, lanes]
            left_t[pl.ds(c * 128, 128), here] = jnp.transpose(part).astype(BF16)

    def give_cov_far(k):
        return remote(
            cov_far.at[pl.ds(k * cov_half, cov_half)],
            cov_relay.at[k],
            cov_sem,
            k,
            dp=dp_next if k == 0 else dp_last,
        )

    def give_cov(k):
        return remote(
            cov_near.at[k], cov_in.at[k], cov_sem, 2 + k, dp=dp_next if k == 0 else dp_last
        )

    def state_relays():
        first_arrived(1, *first_state)
        give_state(5).start()
        first_arrived(2, *first_state)
        give_state(6).start()
        first_arrived(0, *first_state)
        give_state(3).start()
        give_state(4).start()

    def input_cov():
        def take(slot):
            share_hidden(slot).wait_recv()
            give_inverse(slot).wait_recv()
            fill(
                slot,
                lambda lanes: hidden_in[slot - 1, :, lanes],
                column(inverse_in[slot - 1, 0:1, :]),
            )

        give_hidden(3).wait_recv()
        give_hidden(7).start()
        share_hidden(5).start()
        give_hidden(4).wait_recv()
        give_hidden(8).start()
        share_hidden(6).start()
        give_hidden(5).wait_recv()
        give_hidden(6).wait_recv()
        share_hidden(3).start()
        fill(0, lambda lanes: hidden_ref[:, lanes], inverse_all[...])
        take(1)
        give_state(3).wait_recv()
        give_state(7).start()
        give_state(4).wait_recv()
        give_state(8).start()
        take(2)
        take(4)
        give_hidden(7).wait_recv()
        give_hidden(8).wait_recv()
        share_hidden(7).start()
        give_state(5).wait_recv()
        give_state(6).wait_recv()
        take(3)
        take(5)
        take(6)
        give_state(7).wait_recv()
        give_state(8).wait_recv()
        take(7)

        def block(other):
            lanes = pl.ds(pl.multiple_of(other * block_cols, 128), block_cols)
            part = jnp.dot(left_t[...], rows_all[:, lanes], preferred_element_type=F32)
            part = part * gain_ref[:, lanes]
            return jnp.where(odd == 0, part[:block_rows], part[64 : 64 + block_rows])

        cov_far[...] = block((dp + 2) % dps).astype(BF16)
        give_cov_far(0).start()
        give_cov_far(1).start()
        in_cov_ref[...] = block(dp)
        cov_near[0] = block(dp_next).astype(BF16)
        cov_near[1] = block(dp_last).astype(BF16)

    def cov_relays():
        for k in range(2):
            here = pl.ds(k * cov_half, cov_half)
            give_cov_far(k).wait_recv()
            cov_near[k, here, :] = (
                cov_near[k, here, :].astype(F32) + cov_relay[k].astype(F32)
            ).astype(BF16)
            start(give_cov(k))

    turn_of = jnp.where(has_right, jnp.where(chip > EARLY, 1, 2), 0)

    @pl.loop(0, 3)
    def _(phase):
        @pl.when(phase == turn_of)
        def _():
            backward()

        @pl.when(phase == 0)
        def _():
            state_relays()

        @pl.when(phase == 1)
        def _():
            input_cov()

    cov_relays()

    first_arrived(1, *first_grads)
    start(give_grads(5))
    first_arrived(2, *first_grads)
    start(give_grads(6))
    lend_grads().wait_recv()
    out_rows = out_cov_ref.shape[0]
    for z in range(2):
        lanes = pl.ds(pl.multiple_of(z * (kvw // 2) + (x // 2) * 128, 128), 128)
        for slot in range(3):
            here = pl.ds(slot * rows, rows)
            left_g[z, :, here] = jnp.transpose(grads[here, lanes].astype(F32)).astype(BF16)
    mine = pl.ds(pl.multiple_of((x % 2) * out_rows, 16), out_rows)
    there = pl.ds(0, 3 * rows)
    for z in range(2):
        turned[z] = jnp.dot(left_g[z, mine, there], grads[there, :], preferred_element_type=F32)
    give_grads(5).wait_recv()
    give_grads(6).wait_recv()
    for z in range(2):
        lanes = pl.ds(pl.multiple_of(z * (kvw // 2) + (x // 2) * 128, 128), 128)
        here = pl.ds(3 * rows, rows)
        left_g[z, :, here] = jnp.transpose(grads[here, lanes].astype(F32)).astype(BF16)
        turned[z] += jnp.dot(left_g[z, mine, here], grads[here, :], preferred_element_type=F32)

    def block_of(k):
        z = z_low if k % 2 == 0 else 1 - z_low
        lanes = pl.ds(pl.multiple_of(((dp + k // 2) % dps) * HEAD, 128), HEAD)
        return turned[z, :, lanes]

    def give_out(k):
        return remote(
            out_send.at[k - 1],
            out_recv.at[k - 1],
            out_sem,
            k - 1,
            dp=(dp + k // 2) % dps,
            seq=seq if k % 2 == 0 else z_pair,
        )

    for k in range(1, 2 * dps):
        out_send[k - 1] = block_of(k).astype(BF16)
        start(give_out(k))

    out_cov_ref[...] = block_of(0)
    for k in range(2):
        give_cov(k).wait_recv()
    for k in range(1, 2 * dps):
        give_out(k).wait_recv()

    for copy in sent:
        copy.wait_send()
    for slot in (3, 5, 6, 7):
        share_hidden(slot).wait_send()
    for i in (7, 8):
        give_hidden(i).wait_send()
    for i in range(3, 9):
        give_state(i).wait_send()
    for i in (1, 2):
        for layer in range(CORES):
            first_step(i, layer, *first_grads).wait_send()
    lend_grads().wait_send()
    for i in (3, 4):
        give_hidden(i).wait_send()
    share_hidden(4).wait_send()
    for k in range(2):
        give_cov_far(k).wait_send()

    @pl.when(dp < halves)
    def _():
        for k in range(1, dps):
            give_fold(k, dp).wait_send()

    @pl.when(has_right)
    def _():
        for i in range(PARTS):
            send_forward(i).wait_send()

    @pl.when(has_left)
    def _():
        for i in range(PARTS):
            send_backward(i).wait_send()


def on_device(hidden_in, out_grad, value_weight, norm_gain):
    seqs = lax.axis_size("seq")
    dps = lax.axis_size("dp")
    rows, width = hidden_in.shape[2:]
    window = out_grad.shape[3]
    depth, kvw = value_weight.shape[1:]
    token_count = rows * seqs * dps
    half = rows // CORES
    block = (window // seqs, window // dps)
    out_block = (kvw // seqs, kvw // dps)
    halves = window // depth
    dma = pltpu.SemaphoreType.DMA
    vmem = pl.BlockSpec(memory_space=pltpu.VMEM)
    scratch = [
        pltpu.VMEM((dps - 1, rows, depth), BF16),
        pltpu.VMEM((2, half // 2, depth // CORES), BF16),
        pltpu.VMEM((depth, 128), F32),
        pltpu.VMEM((depth, kvw), BF16),
        pltpu.VMEM((CORES, halves, kvw // halves, kvw), BF16),
        pltpu.VMEM((CORES, kvw, kvw), BF16),
        pltpu.VMEM((rows, kvw), F32),
        pltpu.VMEM((rows, 128), F32),
        pltpu.VMEM((rows, kvw), F32),
        pltpu.VMEM((half, kvw), F32),
        pltpu.VMEM((rows, kvw), BF16),
        pltpu.VMEM((2, half, kvw), BF16),
        pltpu.VMEM((2, rows, kvw), BF16),
        pltpu.VMEM((CORES, 2, half, kvw), BF16),
        pltpu.VMEM((CORES, half, kvw), F32),
        pltpu.VMEM((half, kvw), BF16),
        pltpu.VMEM((half, kvw), BF16),
        pltpu.VMEM((CORES, half, kvw), F32),
        pltpu.VMEM((CORES, half, kvw), F32),
        pltpu.VMEM((CORES, half, 128), F32),
        pltpu.VMEM((CORES, half, kvw), BF16),
        pltpu.VMEM((seqs * rows, kvw), BF16),
        pltpu.VMEM((rows, 128), F32),
        pltpu.VMEM((8, rows), F32),
        pltpu.VMEM((seqs - 1, 8, rows), F32),
        pltpu.VMEM((half, kvw), BF16),
        pltpu.VMEM((half, kvw), BF16),
        pltpu.VMEM((CORES, half, kvw), BF16),
        pltpu.VMEM((RING * rows, kvw), BF16),
        pltpu.VMEM((seqs - 1, rows, window), BF16),
        pltpu.VMEM((seqs * rows, window), BF16),
        pltpu.VMEM((384, seqs * rows), BF16),
        pltpu.VMEM(block, BF16),
        pltpu.VMEM((2, block[0] // 2, block[1]), BF16),
        pltpu.VMEM((2,) + block, BF16),
        pltpu.VMEM((2, 128, RING * rows), BF16),
        pltpu.VMEM((2, kvw // seqs, kvw), F32),
        pltpu.VMEM((2 * dps - 1,) + out_block, BF16),
        dma((2, 2)),
        dma((2, 4)),
        dma((2, 3)),
        dma((2, 3)),
        dma((2, 10)),
        dma((2, dps - 1)),
        dma((2,)),
        dma((2, 2)),
        dma((2, CORES, 2, CORES)),
        dma((2, 2, PARTS)),
        dma((2, 3)),
        dma((2, 9)),
        dma((2, seqs - 1)),
        dma((2, 9)),
        dma((2, 3, CORES)),
        dma((2, seqs - 1)),
        dma((2, 9)),
        dma((2, 3, CORES)),
        dma((2, 4)),
        dma((2, 2 * dps - 1)),
    ]
    input_own, input_parts, output_own, output_parts = pl.pallas_call(
        kernel,
        out_shape=(
            jax.ShapeDtypeStruct(block, F32),
            jax.ShapeDtypeStruct((2,) + block, BF16),
            jax.ShapeDtypeStruct(out_block, F32),
            jax.ShapeDtypeStruct((2 * dps - 1,) + out_block, BF16),
        ),
        in_specs=[vmem] * 4,
        out_specs=(vmem,) * 4,
        scratch_shapes=scratch,
        compiler_params=pltpu.CompilerParams(
            collective_id=0, has_side_effects=True, vmem_limit_bytes=56 * 1024 * 1024
        ),
    )(
        hidden_in.reshape(rows, width),
        out_grad.reshape(rows, window),
        value_weight.reshape(depth, kvw),
        norm_gain,
    )
    input_cov = input_own + (input_parts[0].astype(F32) + input_parts[1].astype(F32))
    output_cov = output_own + jnp.sum(output_parts.astype(F32), axis=0)
    return (input_cov[None] / token_count, output_cov.T[None] / token_count)


def solution(mesh):
    return jax.shard_map(
        on_device,
        mesh=mesh,
        in_specs=(
            P(None, "dp", "seq", None),
            P(None, "dp", "seq", None),
            P("section", "dp", None),
            P("section", None),
        ),
        out_specs=(P("section", "seq", "dp"), P("section", "dp", "seq")),
        check_vma=False,
    )
```

```python
import functools

import jax
import jax.numpy as jnp
from jax import lax
from jax.experimental import pallas as pl
from jax.experimental.pallas import tpu as pltpu
from jax.sharding import PartitionSpec as P

HEAD = 128
GROUP = 5
CORES = 2
RING = 4
PARTS = 4
AHEAD = 4
EARLY = 4

epsilon = 1e-06

MESH = pl.DeviceIdType.MESH
F32 = jnp.float32
BF16 = jnp.bfloat16


def column(row):
    return jnp.transpose(jnp.broadcast_to(row, (128, 128)))


def kernel(
    hidden_ref,
    grad_ref,
    weight_ref,
    gain_ref,
    in_cov_ref,
    cov_in,
    out_cov_ref,
    out_recv,
    crossed,
    relayed,
    gain_col,
    scaled,
    cmat,
    cmat_t,
    mean5,
    spare,
    own_out,
    own_in,
    far_out,
    far_in,
    near_out,
    near_in,
    base,
    chain_in,
    chain_out,
    centred,
    product,
    inverse,
    states,
    state,
    inverse_all,
    inverse_row,
    inverse_in,
    grad_in,
    grad_out,
    dvalues,
    grads,
    hidden_in,
    rows_all,
    left_t,
    cov_far,
    cov_relay,
    cov_near,
    left_g,
    turned,
    out_send,
    cross_sem,
    relay_sem,
    pair_sem,
    share_sem,
    cmat_sem,
    fold_sem,
    own_sem,
    far_sem,
    near_sem,
    chain_sem,
    lend_sem,
    hidden_sem,
    hidden_share,
    state_sem,
    state_first,
    inverse_sem,
    grads_sem,
    grads_first,
    cov_sem,
    out_sem,
):
    section = lax.axis_index("section")
    seq = lax.axis_index("seq")
    dp = lax.axis_index("dp")
    sections = lax.axis_size("section")
    seqs = lax.axis_size("seq")
    dps = lax.axis_size("dp")
    rows, width = hidden_ref.shape
    window = grad_ref.shape[1]
    depth, kvw = weight_ref.shape
    heads = kvw // HEAD
    chip = section // CORES
    core = section % CORES
    sibling = chip * CORES + (1 - core)
    has_left = chip > 0
    has_right = chip < sections // CORES - 1
    x = seq % RING
    z_low = seq // RING
    x_next = z_low * RING + (x + 1) % RING
    x_last = z_low * RING + (x + RING - 1) % RING
    z_pair = (1 - z_low) * RING + x
    dp_next = (dp + 1) % dps
    dp_last = (dp + dps - 1) % dps
    half = rows // CORES
    step = half // PARTS

    sent = []

    def remote(src, dst, sem, *index, **device):
        return pltpu.make_async_remote_copy(
            src_ref=src,
            dst_ref=dst,
            send_sem=sem.at[(0,) + index],
            recv_sem=sem.at[(1,) + index],
            device_id=device,
            device_id_type=MESH,
        )

    def start(copy):
        copy.start()
        sent.append(copy)

    barrier = pltpu.get_barrier_semaphore()

    def greet(**device):
        pl.semaphore_signal(barrier, inc=1, device_id=device, device_id_type=MESH)

    for k in range(1, dps):
        greet(dp=(dp + k) % dps)
        greet(dp=(dp + k) % dps, seq=z_pair)
    for j in range(1, seqs):
        greet(seq=seq ^ j)
    greet(section=sibling)
    greet(section=sibling, dp=dp_next)
    greet(section=sibling, dp=dp_last)
    for other in (z_pair, x_next, x_last):
        greet(section=sibling, seq=other)

    @pl.when(has_left)
    def _():
        greet(section=section - CORES)

    @pl.when(has_right)
    def _():
        greet(section=section + CORES)

    pl.semaphore_wait(
        barrier,
        2 * (dps - 1) + seqs - 1 + 6 + has_left.astype(jnp.int32) + has_right.astype(jnp.int32),
    )

    piece = depth // CORES
    my_piece = pl.ds(pl.multiple_of(core * piece, 128), piece)
    side = chip % 2
    pair = section + CORES - 2 * CORES * side
    quarter = half // 2
    my_half = pl.ds(pl.multiple_of(side * half, 16), half)

    def columns_of(other):
        return pl.ds(pl.multiple_of(other * depth + core * piece, 128), piece)

    def cross(k):
        other = dp_next if k == 0 else dp_last
        return remote(
            hidden_ref.at[my_half, columns_of(other)],
            crossed.at[2 * k, my_half, my_piece],
            cross_sem,
            k,
            dp=other,
        )

    far_columns = columns_of((dp + 2) % dps)

    def my_quarter(k):
        return pl.ds(pl.multiple_of(side * half + k * quarter, 16), quarter)

    def far_first(k):
        return remote(
            hidden_ref.at[my_quarter(k), far_columns],
            relayed.at[k],
            relay_sem,
            k,
            dp=dp_next if k == 0 else dp_last,
        )

    def far_second(k):
        return remote(
            relayed.at[k],
            crossed.at[1, my_quarter(k), my_piece],
            relay_sem,
            2 + k,
            dp=dp_next if k == 0 else dp_last,
        )

    def share_pair(slot):
        where = crossed.at[slot, my_half, my_piece]
        return remote(where, where, pair_sem, slot, section=pair)

    def share(slot):
        return remote(
            crossed.at[slot, :, my_piece],
            crossed.at[slot, :, my_piece],
            share_sem,
            slot,
            section=sibling,
        )

    start(far_first(0))
    start(far_first(1))
    start(cross(0))
    start(cross(1))

    first = pl.multiple_of(dp * depth, 128)

    @pl.loop(0, depth // HEAD)
    def _(block):
        where = pl.ds(pl.multiple_of(block * HEAD, HEAD), HEAD)
        gain_here = column(gain_ref[:, pl.ds(pl.multiple_of(first + block * HEAD, HEAD), HEAD)])
        gain_col[where, :] = gain_here

    halves = window // depth
    fold_rows = kvw // halves
    chunk = fold_rows // seqs
    fold_here = pl.ds(pl.multiple_of(seq * chunk, 16), chunk)

    def give_fold(k, part):
        where = cmat.at[core, part, fold_here]
        return pltpu.make_async_remote_copy(
            src_ref=where,
            dst_ref=where,
            send_sem=fold_sem.at[0, k - 1],
            recv_sem=fold_sem.at[1, part],
            device_id={"dp": (dp + k) % dps},
            device_id_type=MESH,
        )

    def share_cmat():
        return remote(cmat.at[core], cmat.at[core], cmat_sem, 9, section=sibling)

    @pl.when(dp < halves)
    def _():
        per_head = HEAD // chunk
        row = (seq // per_head) * (GROUP * HEAD) + (seq % per_head) * chunk
        for c in range(kvw // 128):
            lanes = pl.ds(c * 128, 128)
            total = None
            for q in range(GROUP):
                where = pl.ds(pl.multiple_of(row + q * HEAD, 16), chunk)
                term = weight_ref[where, lanes].astype(F32) * gain_col[where, :]
                total = term if total is None else total + term
            cmat[core, dp, fold_here, lanes] = total.astype(BF16)
        for k in range(1, dps):
            give_fold(k, dp).start()

    for k in range(2):
        far_first(k).wait_recv()
        start(far_second(k))

    @pl.loop(0, depth // HEAD)
    def _(block):
        where = pl.ds(pl.multiple_of(block * HEAD, HEAD), HEAD)
        for c in range(kvw // 128):
            lanes = pl.ds(c * 128, 128)
            scaled[where, lanes] = (
                weight_ref[where, lanes].astype(F32) * gain_col[where, :]
            ).astype(BF16)

    def give_own():
        return remote(
            own_out.at[pl.ds(pl.multiple_of((1 - core) * half, 16), half)],
            own_in,
            own_sem,
            section=sibling,
        )

    own_out[...] = jnp.dot(
        hidden_ref[:, pl.ds(first, depth)], scaled[...], preferred_element_type=F32
    )
    start(give_own())

    def slot_seq(slot):
        z_there = z_low if slot < RING else 1 - z_low
        return z_there * RING + (x + (0, RING - 1, 1, 2)[slot % RING]) % RING

    def ring(sem, view, fixed=False):
        count = chunk if fixed else rows
        front, back = (0, count // 2), (count // 2, count // 2)
        full = (0, count)
        plan = (
            (0, 4, full, z_pair),
            (0, 1, full, x_next),
            (0, 2, full, x_last),
            (4, 5, full, x_next),
            (4, 6, full, x_last),
            (1, 3, front, x_next),
            (2, 3, back, x_last),
            (5, 7, front, x_next),
            (6, 7, back, x_last),
        )

        def copy(i):
            src, dst, part, device = plan[i]
            source = view(src, *part)
            return remote(source, source if fixed else view(dst, *part), sem, i, seq=device)

        return copy

    wide = window // CORES
    my_wide = pl.ds(pl.multiple_of(core * wide, 128), wide)

    def hidden_view(slot, low, count):
        if slot == 0:
            return hidden_ref.at[pl.ds(low, count), my_wide]
        return hidden_in.at[slot - 1, pl.ds(low, count), my_wide]

    def share_hidden(slot):
        where = hidden_in.at[slot - 1, :, my_wide]
        return remote(where, where, hidden_share, slot - 1, section=sibling)

    def cmat_view(slot, low, count):
        begin = slot_seq(slot) * chunk + low
        return cmat.at[core, :, pl.ds(pl.multiple_of(begin, 16), count)]

    give_cmat = ring(cmat_sem, cmat_view, True)
    give_hidden = ring(hidden_sem, hidden_view)
    give_state = ring(state_sem, lambda slot, low, count: state.at[pl.ds(slot * rows + low, count)])
    give_grads = ring(grads_sem, lambda slot, low, count: grads.at[pl.ds(slot * rows + low, count)])

    def give_inverse(slot):
        z_there = z_low if slot < RING else 1 - z_low
        x_there = (x + (0, 1, 3, 2)[slot % RING]) % RING
        return remote(
            inverse_row,
            inverse_in.at[slot - 1],
            inverse_sem,
            slot - 1,
            seq=z_there * RING + x_there,
        )


    cross(0).wait_recv()
    start(share_pair(0))
    cross(1).wait_recv()
    start(share_pair(2))
    for part in range(halves):

        @pl.when(dp != part)
        def _():
            give_fold(1, part).wait_recv()

    for i in range(3):
        start(give_cmat(i))
    for k in range(2):
        far_second(k).wait_recv()
    start(share_pair(1))
    for slot in (0, 2):
        share_pair(slot).wait_recv()
        start(share(slot))
    share_pair(1).wait_recv()
    start(share(1))

    def partial_rows(slot):
        share(slot).wait_recv()
        return jnp.dot(crossed[slot], scaled[...], preferred_element_type=F32)

    def give_far(k):
        return remote(
            far_out.at[pl.ds(k * half, half)],
            far_in.at[k],
            far_sem,
            k,
            dp=dp_next if k == 0 else dp_last,
        )

    def give_near(way, other_core):
        return remote(
            near_out.at[way, pl.ds(other_core * half, half)],
            near_in.at[core, way],
            near_sem,
            core,
            way,
            other_core,
            dp=dp_next if way == 0 else dp_last,
            section=chip * CORES + other_core,
        )

    def near_arrived(layer, way):
        where = near_in.at[layer, way]
        pltpu.make_async_remote_copy(
            src_ref=where,
            dst_ref=where,
            send_sem=near_sem.at[0, layer, way, core],
            recv_sem=near_sem.at[1, layer, way, core],
            device_id={"dp": dp_next},
            device_id_type=MESH,
        ).wait_recv()

    near_last = partial_rows(0)
    near_out[1, pl.ds(0, half), :] = near_last[:half].astype(BF16)
    start(give_near(1, 0))
    near_next = partial_rows(2)
    near_out[0, pl.ds(half, half), :] = near_next[half:].astype(BF16)
    start(give_near(0, 1))
    for i, onward in ((0, (3, 4)), (1, (5,)), (2, (6,))):
        give_cmat(i).wait_recv()
        for j in onward:
            start(give_cmat(j))
    far_out[...] = partial_rows(1).astype(BF16)
    start(give_far(0))
    start(give_far(1))
    for i in (3, 4):
        give_cmat(i).wait_recv()
        start(give_cmat(i + 4))
    start(give_hidden(1))
    start(give_hidden(2))

    fixed = jnp.zeros((rows, HEAD), F32)
    for k in range(heads):
        parts = [
            hidden_ref[:, pl.ds((k * GROUP + q) * HEAD, HEAD)].astype(F32) for q in range(GROUP)
        ]
        mean = (parts[0] + parts[1] + parts[2] + parts[3] + parts[4]) * (1.0 / GROUP)
        mean5[:, pl.ds(k * HEAD, HEAD)] = mean
        for part in parts:
            fixed = fixed + (part - mean) * (part - mean)
    for b in range(window // HEAD, width // HEAD):
        part = hidden_ref[:, pl.ds(b * HEAD, HEAD)].astype(F32)
        fixed = fixed + part * part
    spare[...] = jnp.broadcast_to(jnp.sum(fixed, axis=1, keepdims=True), (rows, 128))

    my_rows = pl.ds(pl.multiple_of(core * half, 16), half)

    @pl.when(chip == 0)
    def _():
        chain_in[...] = jnp.zeros((half, kvw), BF16)

    @pl.when(jnp.logical_not(has_right))
    def _():
        for k in range(heads):
            total = grad_ref[my_rows, pl.ds(k * GROUP * HEAD, HEAD)].astype(F32)
            for q in range(1, GROUP):
                total = total + grad_ref[my_rows, pl.ds((k * GROUP + q) * HEAD, HEAD)].astype(F32)
            grad_in[:, pl.ds(k * HEAD, HEAD)] = total.astype(BF16)

    for i in range(5, 9):
        give_cmat(i).wait_recv()
    start(share_cmat())

    give_far(0).wait_recv()
    near_out[0, pl.ds(0, half), :] = (near_next[:half] + far_in[0].astype(F32)).astype(BF16)
    start(give_near(0, 0))
    give_far(1).wait_recv()
    near_out[1, pl.ds(half, half), :] = (near_last[half:] + far_in[1].astype(F32)).astype(BF16)
    start(give_near(1, 1))

    start(give_hidden(0))
    give_hidden(1).wait_recv()
    start(give_hidden(5))
    start(share_hidden(1))
    give_hidden(2).wait_recv()
    start(give_hidden(6))
    start(share_hidden(2))

    share_cmat().wait_recv()
    for layer in range(CORES):
        cmat_t[layer] = jnp.transpose(cmat[layer].reshape(kvw, kvw))

    give_own().wait_recv()
    for layer in range(CORES):
        near_arrived(layer, 0)
        near_arrived(layer, 1)
        own = jnp.where(core == layer, own_out[my_rows, :], own_in[...])
        base[layer] = own + (near_in[layer, 0].astype(F32) + near_in[layer, 1].astype(F32))

    def pass_hidden():
        give_hidden(0).wait_recv()
        give_hidden(3).start()
        give_hidden(4).start()
        share_hidden(4).start()

    def pass_hidden_on():
        give_hidden(3).wait_recv()
        give_hidden(7).start()
        share_hidden(5).start()
        give_hidden(4).wait_recv()
        give_hidden(8).start()
        share_hidden(6).start()
        give_hidden(5).wait_recv()
        give_hidden(6).wait_recv()
        share_hidden(3).start()

    @pl.when(chip >= AHEAD)
    def _():
        pass_hidden()

    @pl.when(chip >= AHEAD + 2)
    def _():
        pass_hidden_on()

    def send_forward(i):
        where = pl.ds(i * step, step)
        return remote(
            chain_out.at[where], chain_in.at[where], chain_sem, 0, i, section=section + CORES
        )

    def send_backward(i):
        where = pl.ds(i * step, step)
        return remote(
            grad_out.at[where], grad_in.at[where], chain_sem, 1, i, section=section - CORES
        )

    for i in range(PARTS):
        where = pl.ds(i * step, step)
        here = pl.ds(pl.multiple_of(core * half + i * step, 16), step)

        @pl.when(has_left)
        def _():
            send_forward(i).wait_recv()

        s = chain_in[where, :]
        s32 = s.astype(F32)
        for layer in range(CORES):
            c32 = s32 + mean5[here, :]
            squares = spare[here, 0:1] + GROUP * jnp.sum(c32 * c32, axis=1, keepdims=True)
            inv = lax.rsqrt(squares * (1.0 / width) + epsilon)
            prod = (
                jnp.dot(s, cmat[layer].reshape(kvw, kvw), preferred_element_type=F32)
                + base[layer, where, :]
            )
            states[layer, where, :] = s
            centred[layer, where, :] = c32
            product[layer, where, :] = prod
            inverse[layer, where, :] = jnp.broadcast_to(inv, (step, 128))
            s32 = s32 + inv * prod
            s = s32.astype(BF16)
        chain_out[where, :] = s

        @pl.when(has_right)
        def _():
            send_forward(i).start()

    def lend_state():
        return remote(states.at[1 - core], state.at[my_rows], lend_sem, 0, section=sibling)

    def lend_inverse():
        return remote(inverse.at[1 - core], inverse_all.at[my_rows], lend_sem, 1, section=sibling)

    def lend_grads():
        return remote(dvalues.at[1 - core], grads.at[my_rows], lend_sem, 2, section=sibling)

    def first_step(i, layer, source, target, sem):
        slot = (4, 1, 2)[i]
        where = pl.ds(pl.multiple_of(slot * rows + core * half, 16), half)
        return pltpu.make_async_remote_copy(
            src_ref=source.at[layer],
            dst_ref=target.at[where],
            send_sem=sem.at[0, i, layer],
            recv_sem=sem.at[1, i, core],
            device_id={"section": chip * CORES + layer, "seq": (z_pair, x_next, x_last)[i]},
            device_id_type=MESH,
        )

    def first_arrived(i, source, target, sem):
        for other in range(CORES):
            where = target.at[pl.ds((4, 1, 2)[i] * rows + other * half, half)]
            pltpu.make_async_remote_copy(
                src_ref=where,
                dst_ref=where,
                send_sem=sem.at[0, i, other],
                recv_sem=sem.at[1, i, other],
                device_id={"seq": x_next},
                device_id_type=MESH,
            ).wait_recv()

    first_state = (states, state, state_first)
    first_grads = (dvalues, grads, grads_first)

    for i in (1, 2, 0):
        for layer in range(CORES):
            start(first_step(i, layer, *first_state))
    start(lend_inverse())
    start(lend_state())
    state[my_rows, :] = states[core]
    inverse_all[my_rows, :] = inverse[core]
    lend_inverse().wait_recv()
    inverse_row[...] = jnp.transpose(inverse_all[...])[0:8, :]
    for slot in range(1, seqs):
        start(give_inverse(slot))
    lend_state().wait_recv()

    @pl.when(chip < AHEAD)
    def _():
        pass_hidden()

    def backward():
        for i in range(PARTS):
            where = pl.ds(i * step, step)

            @pl.when(has_right)
            def _():
                send_backward(i).wait_recv()

            def turn(g, g32, layer):
                other = jnp.dot(g, cmat_t[layer], preferred_element_type=F32)
                inner = jnp.sum(g32 * product[layer, where, :], axis=1, keepdims=True)
                inv = inverse[layer, where, 0:1]
                factor = inv * inv * inner * (GROUP / width)
                return g32 + inv * (other - centred[layer, where, :] * factor)

            g = grad_in[where, :]
            dvalues[1, where, :] = g
            g32 = turn(g, g.astype(F32), 1)
            g = g32.astype(BF16)
            dvalues[0, where, :] = g

            @pl.when(has_left)
            def _():
                grad_out[where, :] = turn(g, g.astype(F32), 0).astype(BF16)
                send_backward(i).start()

        for i in (1, 2):
            for layer in range(CORES):
                first_step(i, layer, *first_grads).start()
        lend_grads().start()
        grads[my_rows, :] = dvalues[core]

    begin = pl.multiple_of((seq // 2) * (GROUP * HEAD) + (seq % 2) * 256, 128)
    odd = seq % 2
    block_rows, block_cols = in_cov_ref.shape
    cov_half = block_rows // 2

    def fill(slot, read_hidden, inv):
        here = pl.ds(slot * rows, rows)
        for k in range(heads):
            s32 = state[here, pl.ds(k * HEAD, HEAD)].astype(F32)
            for q in range(GROUP):
                lanes = pl.ds((k * GROUP + q) * HEAD, HEAD)
                rows_all[here, lanes] = (read_hidden(lanes).astype(F32) + s32).astype(BF16)
        factor = inv * inv
        for c in range(3):
            lanes = pl.ds(pl.multiple_of(begin + c * 128, 128), 128)
            part = rows_all[here, lanes].astype(F32) * factor * gain_ref[:, lanes]
            left_t[pl.ds(c * 128, 128), here] = jnp.transpose(part).astype(BF16)

    def give_cov_far(k):
        return remote(
            cov_far.at[pl.ds(k * cov_half, cov_half)],
            cov_relay.at[k],
            cov_sem,
            k,
            dp=dp_next if k == 0 else dp_last,
        )

    def give_cov(k, part):
        where = pl.ds(part * cov_half, cov_half)
        return remote(
            cov_near.at[k, where],
            cov_in.at[k, where],
            cov_sem,
            2 + 2 * k + part,
            dp=dp_next if k == 0 else dp_last,
        )

    def state_relays():
        first_arrived(1, *first_state)
        give_state(5).start()
        first_arrived(2, *first_state)
        give_state(6).start()
        first_arrived(0, *first_state)
        give_state(3).start()
        give_state(4).start()

    def state_relays_on():
        give_state(3).wait_recv()
        give_state(7).start()
        give_state(4).wait_recv()
        give_state(8).start()

        @pl.when(chip < AHEAD + 2)
        def _():
            pass_hidden_on()

    def input_cov():
        def take(slot):
            share_hidden(slot).wait_recv()
            give_inverse(slot).wait_recv()
            fill(
                slot,
                lambda lanes: hidden_in[slot - 1, :, lanes],
                column(inverse_in[slot - 1, 0:1, :]),
            )

        fill(0, lambda lanes: hidden_ref[:, lanes], inverse_all[...])
        take(1)
        take(2)
        take(4)
        give_hidden(7).wait_recv()
        give_hidden(8).wait_recv()
        share_hidden(7).start()
        give_state(5).wait_recv()
        give_state(6).wait_recv()
        take(3)
        take(5)
        take(6)
        give_state(7).wait_recv()
        give_state(8).wait_recv()
        take(7)

        def block(other):
            lanes = pl.ds(pl.multiple_of(other * block_cols, 128), block_cols)
            part = jnp.dot(left_t[...], rows_all[:, lanes], preferred_element_type=F32)
            part = part * gain_ref[:, lanes]
            return jnp.where(odd == 0, part[:block_rows], part[64 : 64 + block_rows])

        cov_far[...] = block((dp + 2) % dps).astype(BF16)
        give_cov_far(0).start()
        give_cov_far(1).start()
        in_cov_ref[...] = block(dp)
        cov_near[0] = block(dp_next).astype(BF16)
        cov_near[1] = block(dp_last).astype(BF16)

    def cov_relays():
        for k in range(2):
            give_cov_far(k).wait_send()
            start(give_cov(k, 1 - k))
        for k in range(2):
            here = pl.ds(k * cov_half, cov_half)
            give_cov_far(k).wait_recv()
            cov_near[k, here, :] = (
                cov_near[k, here, :].astype(F32) + cov_relay[k].astype(F32)
            ).astype(BF16)
            start(give_cov(k, k))

    turn_of = jnp.where(chip > EARLY, sections // CORES - 1 - chip, 3)

    @pl.loop(0, 4)
    def _(phase):
        @pl.when(phase == turn_of)
        def _():
            backward()

        @pl.when(phase == 0)
        def _():
            state_relays()

        @pl.when(phase == 1)
        def _():
            state_relays_on()

        @pl.when(phase == 2)
        def _():
            input_cov()

    cov_relays()

    first_arrived(1, *first_grads)
    start(give_grads(5))
    first_arrived(2, *first_grads)
    start(give_grads(6))
    lend_grads().wait_recv()
    out_rows = out_cov_ref.shape[0]
    for z in range(2):
        lanes = pl.ds(pl.multiple_of(z * (kvw // 2) + (x // 2) * 128, 128), 128)
        for slot in range(3):
            here = pl.ds(slot * rows, rows)
            left_g[z, :, here] = jnp.transpose(grads[here, lanes].astype(F32)).astype(BF16)
    mine = pl.ds(pl.multiple_of((x % 2) * out_rows, 16), out_rows)
    there = pl.ds(0, 3 * rows)
    for z in range(2):
        turned[z] = jnp.dot(left_g[z, mine, there], grads[there, :], preferred_element_type=F32)
    give_grads(5).wait_recv()
    give_grads(6).wait_recv()
    for z in range(2):
        lanes = pl.ds(pl.multiple_of(z * (kvw // 2) + (x // 2) * 128, 128), 128)
        here = pl.ds(3 * rows, rows)
        left_g[z, :, here] = jnp.transpose(grads[here, lanes].astype(F32)).astype(BF16)
        turned[z] += jnp.dot(left_g[z, mine, here], grads[here, :], preferred_element_type=F32)

    def block_of(k):
        z = z_low if k % 2 == 0 else 1 - z_low
        lanes = pl.ds(pl.multiple_of(((dp + k // 2) % dps) * HEAD, 128), HEAD)
        return turned[z, :, lanes]

    def give_out(k):
        return remote(
            out_send.at[k - 1],
            out_recv.at[k - 1],
            out_sem,
            k - 1,
            dp=(dp + k // 2) % dps,
            seq=seq if k % 2 == 0 else z_pair,
        )

    for k in range(1, 2 * dps):
        out_send[k - 1] = block_of(k).astype(BF16)
        start(give_out(k))

    out_cov_ref[...] = block_of(0)
    for k in range(2):
        for part in range(2):
            give_cov(k, part).wait_recv()
    for k in range(1, 2 * dps):
        give_out(k).wait_recv()

    for copy in sent:
        copy.wait_send()
    for slot in (3, 5, 6, 7):
        share_hidden(slot).wait_send()
    for i in (7, 8):
        give_hidden(i).wait_send()
    for i in range(3, 9):
        give_state(i).wait_send()
    for i in (1, 2):
        for layer in range(CORES):
            first_step(i, layer, *first_grads).wait_send()
    lend_grads().wait_send()
    for i in (3, 4):
        give_hidden(i).wait_send()
    share_hidden(4).wait_send()

    @pl.when(dp < halves)
    def _():
        for k in range(1, dps):
            give_fold(k, dp).wait_send()

    @pl.when(has_right)
    def _():
        for i in range(PARTS):
            send_forward(i).wait_send()

    @pl.when(has_left)
    def _():
        for i in range(PARTS):
            send_backward(i).wait_send()


def add_parts(scale, input_own, input_parts, output_own, output_parts, input_cov, output_cov):
    total = input_own[...] + (input_parts[0].astype(F32) + input_parts[1].astype(F32))
    input_cov[...] = total * scale
    total = output_own[...]
    for k in range(output_parts.shape[0]):
        total = total + output_parts[k].astype(F32)
    output_cov[...] = total * scale


def on_device(hidden_in, out_grad, value_weight, norm_gain):
    seqs = lax.axis_size("seq")
    dps = lax.axis_size("dp")
    rows, width = hidden_in.shape[2:]
    window = out_grad.shape[3]
    depth, kvw = value_weight.shape[1:]
    token_count = rows * seqs * dps
    half = rows // CORES
    block = (window // seqs, window // dps)
    out_block = (kvw // seqs, kvw // dps)
    halves = window // depth
    dma = pltpu.SemaphoreType.DMA
    vmem = pl.BlockSpec(memory_space=pltpu.VMEM)
    scratch = [
        pltpu.VMEM((dps - 1, rows, depth), BF16),
        pltpu.VMEM((2, half // 2, depth // CORES), BF16),
        pltpu.VMEM((depth, 128), F32),
        pltpu.VMEM((depth, kvw), BF16),
        pltpu.VMEM((CORES, halves, kvw // halves, kvw), BF16),
        pltpu.VMEM((CORES, kvw, kvw), BF16),
        pltpu.VMEM((rows, kvw), F32),
        pltpu.VMEM((rows, 128), F32),
        pltpu.VMEM((rows, kvw), F32),
        pltpu.VMEM((half, kvw), F32),
        pltpu.VMEM((rows, kvw), BF16),
        pltpu.VMEM((2, half, kvw), BF16),
        pltpu.VMEM((2, rows, kvw), BF16),
        pltpu.VMEM((CORES, 2, half, kvw), BF16),
        pltpu.VMEM((CORES, half, kvw), F32),
        pltpu.VMEM((half, kvw), BF16),
        pltpu.VMEM((half, kvw), BF16),
        pltpu.VMEM((CORES, half, kvw), F32),
        pltpu.VMEM((CORES, half, kvw), F32),
        pltpu.VMEM((CORES, half, 128), F32),
        pltpu.VMEM((CORES, half, kvw), BF16),
        pltpu.VMEM((seqs * rows, kvw), BF16),
        pltpu.VMEM((rows, 128), F32),
        pltpu.VMEM((8, rows), F32),
        pltpu.VMEM((seqs - 1, 8, rows), F32),
        pltpu.VMEM((half, kvw), BF16),
        pltpu.VMEM((half, kvw), BF16),
        pltpu.VMEM((CORES, half, kvw), BF16),
        pltpu.VMEM((RING * rows, kvw), BF16),
        pltpu.VMEM((seqs - 1, rows, window), BF16),
        pltpu.VMEM((seqs * rows, window), BF16),
        pltpu.VMEM((384, seqs * rows), BF16),
        pltpu.VMEM(block, BF16),
        pltpu.VMEM((2, block[0] // 2, block[1]), BF16),
        pltpu.VMEM((2,) + block, BF16),
        pltpu.VMEM((2, 128, RING * rows), BF16),
        pltpu.VMEM((2, kvw // seqs, kvw), F32),
        pltpu.VMEM((2 * dps - 1,) + out_block, BF16),
        dma((2, 2)),
        dma((2, 4)),
        dma((2, 3)),
        dma((2, 3)),
        dma((2, 10)),
        dma((2, dps - 1)),
        dma((2,)),
        dma((2, 2)),
        dma((2, CORES, 2, CORES)),
        dma((2, 2, PARTS)),
        dma((2, 3)),
        dma((2, 9)),
        dma((2, seqs - 1)),
        dma((2, 9)),
        dma((2, 3, CORES)),
        dma((2, seqs - 1)),
        dma((2, 9)),
        dma((2, 3, CORES)),
        dma((2, 6)),
        dma((2, 2 * dps - 1)),
    ]
    input_own, input_parts, output_own, output_parts = pl.pallas_call(
        kernel,
        out_shape=(
            jax.ShapeDtypeStruct(block, F32),
            jax.ShapeDtypeStruct((2,) + block, BF16),
            jax.ShapeDtypeStruct(out_block, F32),
            jax.ShapeDtypeStruct((2 * dps - 1,) + out_block, BF16),
        ),
        in_specs=[vmem] * 4,
        out_specs=(vmem,) * 4,
        scratch_shapes=scratch,
        compiler_params=pltpu.CompilerParams(
            collective_id=0, has_side_effects=True, vmem_limit_bytes=56 * 1024 * 1024
        ),
    )(
        hidden_in.reshape(rows, width),
        out_grad.reshape(rows, window),
        value_weight.reshape(depth, kvw),
        norm_gain,
    )
    input_cov, output_cov = pl.pallas_call(
        functools.partial(add_parts, 1.0 / token_count),
        out_shape=(
            jax.ShapeDtypeStruct(block, F32),
            jax.ShapeDtypeStruct(out_block, F32),
        ),
        in_specs=[vmem] * 4,
        out_specs=(vmem,) * 2,
    )(input_own, input_parts, output_own, output_parts)
    return (input_cov[None], output_cov.T[None])


def solution(mesh):
    return jax.shard_map(
        on_device,
        mesh=mesh,
        in_specs=(
            P(None, "dp", "seq", None),
            P(None, "dp", "seq", None),
            P("section", "dp", None),
            P("section", None),
        ),
        out_specs=(P("section", "seq", "dp"), P("section", "dp", "seq")),
        check_vma=False,
    )
```

```python
import functools

import jax
import jax.numpy as jnp
from jax import lax
from jax.experimental import pallas as pl
from jax.experimental.pallas import tpu as pltpu
from jax.sharding import PartitionSpec as P

HEAD = 128
GROUP = 5
CORES = 2
RING = 4
PARTS = 4
AHEAD = 4
EARLY = 4

epsilon = 1e-06

MESH = pl.DeviceIdType.MESH
F32 = jnp.float32
BF16 = jnp.bfloat16


def column(row):
    return jnp.transpose(jnp.broadcast_to(row, (128, 128)))


def kernel(
    hidden_arg,
    grad_arg,
    weight_arg,
    gain_ref,
    in_cov_ref,
    cov_in,
    out_cov_ref,
    out_recv,
    hidden_ref,
    grad_ref,
    weight_ref,
    crossed,
    relayed,
    gain_col,
    scaled,
    cmat,
    cmat_t,
    mean5,
    spare,
    own_out,
    own_in,
    far_out,
    far_in,
    near_out,
    near_in,
    base,
    chain_in,
    chain_out,
    centred,
    product,
    inverse,
    states,
    state,
    inverse_all,
    inverse_row,
    inverse_in,
    grad_in,
    grad_out,
    dvalues,
    grads,
    hidden_in,
    rows_all,
    left_t,
    cov_far,
    cov_relay,
    cov_near,
    left_g,
    turned,
    out_send,
    load_sem,
    cross_sem,
    relay_sem,
    pair_sem,
    share_sem,
    cmat_sem,
    fold_sem,
    own_sem,
    far_sem,
    near_sem,
    chain_sem,
    lend_sem,
    hidden_sem,
    hidden_share,
    state_sem,
    state_first,
    inverse_sem,
    grads_sem,
    grads_first,
    cov_sem,
    out_sem,
):
    section = lax.axis_index("section")
    seq = lax.axis_index("seq")
    dp = lax.axis_index("dp")
    sections = lax.axis_size("section")
    seqs = lax.axis_size("seq")
    dps = lax.axis_size("dp")
    rows, width = hidden_ref.shape
    window = grad_ref.shape[1]
    depth, kvw = weight_ref.shape
    heads = kvw // HEAD
    chip = section // CORES
    core = section % CORES
    sibling = chip * CORES + (1 - core)
    has_left = chip > 0
    has_right = chip < sections // CORES - 1
    x = seq % RING
    z_low = seq // RING
    x_next = z_low * RING + (x + 1) % RING
    x_last = z_low * RING + (x + RING - 1) % RING
    z_pair = (1 - z_low) * RING + x
    dp_next = (dp + 1) % dps
    dp_last = (dp + dps - 1) % dps
    half = rows // CORES
    step = half // PARTS

    sent = []

    def remote(src, dst, sem, *index, **device):
        return pltpu.make_async_remote_copy(
            src_ref=src,
            dst_ref=dst,
            send_sem=sem.at[(0,) + index],
            recv_sem=sem.at[(1,) + index],
            device_id=device,
            device_id_type=MESH,
        )

    def start(copy):
        copy.start()
        sent.append(copy)

    loads = [
        pltpu.make_async_copy(source, target, load_sem.at[i])
        for i, (source, target) in enumerate(
            ((hidden_arg, hidden_ref), (weight_arg, weight_ref), (grad_arg, grad_ref))
        )
    ]
    for load in loads:
        load.start()

    barrier = pltpu.get_barrier_semaphore()

    def greet(**device):
        pl.semaphore_signal(barrier, inc=1, device_id=device, device_id_type=MESH)

    for k in range(1, dps):
        greet(dp=(dp + k) % dps)
        greet(dp=(dp + k) % dps, seq=z_pair)
    for j in range(1, seqs):
        greet(seq=seq ^ j)
    greet(section=sibling)
    greet(section=sibling, dp=dp_next)
    greet(section=sibling, dp=dp_last)
    for other in (z_pair, x_next, x_last):
        greet(section=sibling, seq=other)

    @pl.when(has_left)
    def _():
        greet(section=section - CORES)

    @pl.when(has_right)
    def _():
        greet(section=section + CORES)

    pl.semaphore_wait(
        barrier,
        2 * (dps - 1) + seqs - 1 + 6 + has_left.astype(jnp.int32) + has_right.astype(jnp.int32),
    )

    piece = depth // CORES
    my_piece = pl.ds(pl.multiple_of(core * piece, 128), piece)
    side = chip % 2
    pair = section + CORES - 2 * CORES * side
    quarter = half // 2
    my_half = pl.ds(pl.multiple_of(side * half, 16), half)

    def columns_of(other):
        return pl.ds(pl.multiple_of(other * depth + core * piece, 128), piece)

    def cross(k):
        other = dp_next if k == 0 else dp_last
        return remote(
            hidden_ref.at[my_half, columns_of(other)],
            crossed.at[2 * k, my_half, my_piece],
            cross_sem,
            k,
            dp=other,
        )

    far_columns = columns_of((dp + 2) % dps)

    def my_quarter(k):
        return pl.ds(pl.multiple_of(side * half + k * quarter, 16), quarter)

    def far_first(k):
        return remote(
            hidden_ref.at[my_quarter(k), far_columns],
            relayed.at[k],
            relay_sem,
            k,
            dp=dp_next if k == 0 else dp_last,
        )

    def far_second(k):
        return remote(
            relayed.at[k],
            crossed.at[1, my_quarter(k), my_piece],
            relay_sem,
            2 + k,
            dp=dp_next if k == 0 else dp_last,
        )

    def share_pair(slot):
        where = crossed.at[slot, my_half, my_piece]
        return remote(where, where, pair_sem, slot, section=pair)

    def share(slot):
        return remote(
            crossed.at[slot, :, my_piece],
            crossed.at[slot, :, my_piece],
            share_sem,
            slot,
            section=sibling,
        )

    loads[0].wait()
    start(far_first(0))
    start(far_first(1))
    start(cross(0))
    start(cross(1))

    first = pl.multiple_of(dp * depth, 128)

    @pl.loop(0, depth // HEAD)
    def _(block):
        where = pl.ds(pl.multiple_of(block * HEAD, HEAD), HEAD)
        gain_here = column(gain_ref[:, pl.ds(pl.multiple_of(first + block * HEAD, HEAD), HEAD)])
        gain_col[where, :] = gain_here

    halves = window // depth
    fold_rows = kvw // halves
    chunk = fold_rows // seqs
    fold_here = pl.ds(pl.multiple_of(seq * chunk, 16), chunk)

    def give_fold(k, part):
        where = cmat.at[core, part, fold_here]
        return pltpu.make_async_remote_copy(
            src_ref=where,
            dst_ref=where,
            send_sem=fold_sem.at[0, k - 1],
            recv_sem=fold_sem.at[1, part],
            device_id={"dp": (dp + k) % dps},
            device_id_type=MESH,
        )

    def share_cmat():
        return remote(cmat.at[core], cmat.at[core], cmat_sem, 9, section=sibling)

    loads[1].wait()

    @pl.when(dp < halves)
    def _():
        per_head = HEAD // chunk
        row = (seq // per_head) * (GROUP * HEAD) + (seq % per_head) * chunk
        for c in range(kvw // 128):
            lanes = pl.ds(c * 128, 128)
            total = None
            for q in range(GROUP):
                where = pl.ds(pl.multiple_of(row + q * HEAD, 16), chunk)
                term = weight_ref[where, lanes].astype(F32) * gain_col[where, :]
                total = term if total is None else total + term
            cmat[core, dp, fold_here, lanes] = total.astype(BF16)
        for k in range(1, dps):
            give_fold(k, dp).start()

    for k in range(2):
        far_first(k).wait_recv()
        start(far_second(k))

    @pl.loop(0, depth // HEAD)
    def _(block):
        where = pl.ds(pl.multiple_of(block * HEAD, HEAD), HEAD)
        for c in range(kvw // 128):
            lanes = pl.ds(c * 128, 128)
            scaled[where, lanes] = (
                weight_ref[where, lanes].astype(F32) * gain_col[where, :]
            ).astype(BF16)

    def give_own():
        return remote(
            own_out.at[pl.ds(pl.multiple_of((1 - core) * half, 16), half)],
            own_in,
            own_sem,
            section=sibling,
        )

    own_out[...] = jnp.dot(
        hidden_ref[:, pl.ds(first, depth)], scaled[...], preferred_element_type=F32
    )
    start(give_own())

    def slot_seq(slot):
        z_there = z_low if slot < RING else 1 - z_low
        return z_there * RING + (x + (0, RING - 1, 1, 2)[slot % RING]) % RING

    def ring(sem, view, fixed=False):
        count = chunk if fixed else rows
        front, back = (0, count // 2), (count // 2, count // 2)
        full = (0, count)
        plan = (
            (0, 4, full, z_pair),
            (0, 1, full, x_next),
            (0, 2, full, x_last),
            (4, 5, full, x_next),
            (4, 6, full, x_last),
            (1, 3, front, x_next),
            (2, 3, back, x_last),
            (5, 7, front, x_next),
            (6, 7, back, x_last),
        )

        def copy(i):
            src, dst, part, device = plan[i]
            source = view(src, *part)
            return remote(source, source if fixed else view(dst, *part), sem, i, seq=device)

        return copy

    wide = window // CORES
    my_wide = pl.ds(pl.multiple_of(core * wide, 128), wide)

    def hidden_view(slot, low, count):
        if slot == 0:
            return hidden_ref.at[pl.ds(low, count), my_wide]
        return hidden_in.at[slot - 1, pl.ds(low, count), my_wide]

    def share_hidden(slot):
        where = hidden_in.at[slot - 1, :, my_wide]
        return remote(where, where, hidden_share, slot - 1, section=sibling)

    def cmat_view(slot, low, count):
        begin = slot_seq(slot) * chunk + low
        return cmat.at[core, :, pl.ds(pl.multiple_of(begin, 16), count)]

    give_cmat = ring(cmat_sem, cmat_view, True)
    give_hidden = ring(hidden_sem, hidden_view)
    give_state = ring(state_sem, lambda slot, low, count: state.at[pl.ds(slot * rows + low, count)])
    give_grads = ring(grads_sem, lambda slot, low, count: grads.at[pl.ds(slot * rows + low, count)])

    def give_inverse(slot):
        z_there = z_low if slot < RING else 1 - z_low
        x_there = (x + (0, 1, 3, 2)[slot % RING]) % RING
        return remote(
            inverse_row,
            inverse_in.at[slot - 1],
            inverse_sem,
            slot - 1,
            seq=z_there * RING + x_there,
        )


    cross(0).wait_recv()
    start(share_pair(0))
    cross(1).wait_recv()
    start(share_pair(2))
    for part in range(halves):

        @pl.when(dp != part)
        def _():
            give_fold(1, part).wait_recv()

    for i in range(3):
        start(give_cmat(i))
    for k in range(2):
        far_second(k).wait_recv()
    start(share_pair(1))
    for slot in (0, 2):
        share_pair(slot).wait_recv()
        start(share(slot))
    share_pair(1).wait_recv()
    start(share(1))

    def partial_rows(slot):
        share(slot).wait_recv()
        return jnp.dot(crossed[slot], scaled[...], preferred_element_type=F32)

    def give_far(k):
        return remote(
            far_out.at[pl.ds(k * half, half)],
            far_in.at[k],
            far_sem,
            k,
            dp=dp_next if k == 0 else dp_last,
        )

    def give_near(way, other_core):
        return remote(
            near_out.at[way, pl.ds(other_core * half, half)],
            near_in.at[core, way],
            near_sem,
            core,
            way,
            other_core,
            dp=dp_next if way == 0 else dp_last,
            section=chip * CORES + other_core,
        )

    def near_arrived(layer, way):
        where = near_in.at[layer, way]
        pltpu.make_async_remote_copy(
            src_ref=where,
            dst_ref=where,
            send_sem=near_sem.at[0, layer, way, core],
            recv_sem=near_sem.at[1, layer, way, core],
            device_id={"dp": dp_next},
            device_id_type=MESH,
        ).wait_recv()

    near_last = partial_rows(0)
    near_out[1, pl.ds(0, half), :] = near_last[:half].astype(BF16)
    start(give_near(1, 0))
    near_next = partial_rows(2)
    near_out[0, pl.ds(half, half), :] = near_next[half:].astype(BF16)
    start(give_near(0, 1))
    for i, onward in ((0, (3, 4)), (1, (5,)), (2, (6,))):
        give_cmat(i).wait_recv()
        for j in onward:
            start(give_cmat(j))
    far_out[...] = partial_rows(1).astype(BF16)
    start(give_far(0))
    start(give_far(1))
    for i in (3, 4):
        give_cmat(i).wait_recv()
        start(give_cmat(i + 4))
    start(give_hidden(1))
    start(give_hidden(2))

    fixed = jnp.zeros((rows, HEAD), F32)
    for k in range(heads):
        parts = [
            hidden_ref[:, pl.ds((k * GROUP + q) * HEAD, HEAD)].astype(F32) for q in range(GROUP)
        ]
        mean = (parts[0] + parts[1] + parts[2] + parts[3] + parts[4]) * (1.0 / GROUP)
        mean5[:, pl.ds(k * HEAD, HEAD)] = mean
        for part in parts:
            fixed = fixed + (part - mean) * (part - mean)
    for b in range(window // HEAD, width // HEAD):
        part = hidden_ref[:, pl.ds(b * HEAD, HEAD)].astype(F32)
        fixed = fixed + part * part
    spare[...] = jnp.broadcast_to(jnp.sum(fixed, axis=1, keepdims=True), (rows, 128))

    my_rows = pl.ds(pl.multiple_of(core * half, 16), half)

    @pl.when(chip == 0)
    def _():
        chain_in[...] = jnp.zeros((half, kvw), BF16)

    loads[2].wait()

    @pl.when(jnp.logical_not(has_right))
    def _():
        for k in range(heads):
            total = grad_ref[my_rows, pl.ds(k * GROUP * HEAD, HEAD)].astype(F32)
            for q in range(1, GROUP):
                total = total + grad_ref[my_rows, pl.ds((k * GROUP + q) * HEAD, HEAD)].astype(F32)
            grad_in[:, pl.ds(k * HEAD, HEAD)] = total.astype(BF16)

    for i in range(5, 9):
        give_cmat(i).wait_recv()
    start(share_cmat())

    give_far(0).wait_recv()
    near_out[0, pl.ds(0, half), :] = (near_next[:half] + far_in[0].astype(F32)).astype(BF16)
    start(give_near(0, 0))
    give_far(1).wait_recv()
    near_out[1, pl.ds(half, half), :] = (near_last[half:] + far_in[1].astype(F32)).astype(BF16)
    start(give_near(1, 1))

    start(give_hidden(0))
    give_hidden(1).wait_recv()
    start(give_hidden(5))
    start(share_hidden(1))
    give_hidden(2).wait_recv()
    start(give_hidden(6))
    start(share_hidden(2))

    share_cmat().wait_recv()
    for layer in range(CORES):
        cmat_t[layer] = jnp.transpose(cmat[layer].reshape(kvw, kvw))

    give_own().wait_recv()
    for layer in range(CORES):
        near_arrived(layer, 0)
        near_arrived(layer, 1)
        own = jnp.where(core == layer, own_out[my_rows, :], own_in[...])
        base[layer] = own + (near_in[layer, 0].astype(F32) + near_in[layer, 1].astype(F32))

    def pass_hidden():
        give_hidden(0).wait_recv()
        give_hidden(3).start()
        give_hidden(4).start()
        share_hidden(4).start()

    def pass_hidden_on():
        give_hidden(3).wait_recv()
        give_hidden(7).start()
        share_hidden(5).start()
        give_hidden(4).wait_recv()
        give_hidden(8).start()
        share_hidden(6).start()
        give_hidden(5).wait_recv()
        give_hidden(6).wait_recv()
        share_hidden(3).start()

    @pl.when(chip >= AHEAD)
    def _():
        pass_hidden()

    @pl.when(chip >= AHEAD + 2)
    def _():
        pass_hidden_on()

    def send_forward(i):
        where = pl.ds(i * step, step)
        return remote(
            chain_out.at[where], chain_in.at[where], chain_sem, 0, i, section=section + CORES
        )

    def send_backward(i):
        where = pl.ds(i * step, step)
        return remote(
            grad_out.at[where], grad_in.at[where], chain_sem, 1, i, section=section - CORES
        )

    for i in range(PARTS):
        where = pl.ds(i * step, step)
        here = pl.ds(pl.multiple_of(core * half + i * step, 16), step)

        @pl.when(has_left)
        def _():
            send_forward(i).wait_recv()

        s = chain_in[where, :]
        s32 = s.astype(F32)
        for layer in range(CORES):
            c32 = s32 + mean5[here, :]
            squares = spare[here, 0:1] + GROUP * jnp.sum(c32 * c32, axis=1, keepdims=True)
            inv = lax.rsqrt(squares * (1.0 / width) + epsilon)
            prod = (
                jnp.dot(s, cmat[layer].reshape(kvw, kvw), preferred_element_type=F32)
                + base[layer, where, :]
            )
            states[layer, where, :] = s
            centred[layer, where, :] = c32
            product[layer, where, :] = prod
            inverse[layer, where, :] = jnp.broadcast_to(inv, (step, 128))
            s32 = s32 + inv * prod
            s = s32.astype(BF16)
        chain_out[where, :] = s

        @pl.when(has_right)
        def _():
            send_forward(i).start()

    def lend_state():
        return remote(states.at[1 - core], state.at[my_rows], lend_sem, 0, section=sibling)

    def lend_inverse():
        return remote(inverse.at[1 - core], inverse_all.at[my_rows], lend_sem, 1, section=sibling)

    def lend_grads():
        return remote(dvalues.at[1 - core], grads.at[my_rows], lend_sem, 2, section=sibling)

    def first_step(i, layer, source, target, sem):
        slot = (4, 1, 2)[i]
        where = pl.ds(pl.multiple_of(slot * rows + core * half, 16), half)
        return pltpu.make_async_remote_copy(
            src_ref=source.at[layer],
            dst_ref=target.at[where],
            send_sem=sem.at[0, i, layer],
            recv_sem=sem.at[1, i, core],
            device_id={"section": chip * CORES + layer, "seq": (z_pair, x_next, x_last)[i]},
            device_id_type=MESH,
        )

    def first_arrived(i, source, target, sem):
        for other in range(CORES):
            where = target.at[pl.ds((4, 1, 2)[i] * rows + other * half, half)]
            pltpu.make_async_remote_copy(
                src_ref=where,
                dst_ref=where,
                send_sem=sem.at[0, i, other],
                recv_sem=sem.at[1, i, other],
                device_id={"seq": x_next},
                device_id_type=MESH,
            ).wait_recv()

    first_state = (states, state, state_first)
    first_grads = (dvalues, grads, grads_first)

    for i in (1, 2, 0):
        for layer in range(CORES):
            start(first_step(i, layer, *first_state))
    start(lend_inverse())
    start(lend_state())
    state[my_rows, :] = states[core]
    inverse_all[my_rows, :] = inverse[core]
    lend_inverse().wait_recv()
    inverse_row[...] = jnp.transpose(inverse_all[...])[0:8, :]
    for slot in range(1, seqs):
        start(give_inverse(slot))
    lend_state().wait_recv()

    @pl.when(chip < AHEAD)
    def _():
        pass_hidden()

    def backward():
        for i in range(PARTS):
            where = pl.ds(i * step, step)

            @pl.when(has_right)
            def _():
                send_backward(i).wait_recv()

            def turn(g, g32, layer):
                other = jnp.dot(g, cmat_t[layer], preferred_element_type=F32)
                inner = jnp.sum(g32 * product[layer, where, :], axis=1, keepdims=True)
                inv = inverse[layer, where, 0:1]
                factor = inv * inv * inner * (GROUP / width)
                return g32 + inv * (other - centred[layer, where, :] * factor)

            g = grad_in[where, :]
            dvalues[1, where, :] = g
            g32 = turn(g, g.astype(F32), 1)
            g = g32.astype(BF16)
            dvalues[0, where, :] = g

            @pl.when(has_left)
            def _():
                grad_out[where, :] = turn(g, g.astype(F32), 0).astype(BF16)
                send_backward(i).start()

        for i in (1, 2):
            for layer in range(CORES):
                first_step(i, layer, *first_grads).start()
        lend_grads().start()
        grads[my_rows, :] = dvalues[core]

    begin = pl.multiple_of((seq // 2) * (GROUP * HEAD) + (seq % 2) * 256, 128)
    odd = seq % 2
    block_rows, block_cols = in_cov_ref.shape
    cov_half = block_rows // 2

    def fill(slot, read_hidden, inv):
        here = pl.ds(slot * rows, rows)
        for k in range(heads):
            s32 = state[here, pl.ds(k * HEAD, HEAD)].astype(F32)
            for q in range(GROUP):
                lanes = pl.ds((k * GROUP + q) * HEAD, HEAD)
                rows_all[here, lanes] = (read_hidden(lanes).astype(F32) + s32).astype(BF16)
        factor = inv * inv
        for c in range(3):
            lanes = pl.ds(pl.multiple_of(begin + c * 128, 128), 128)
            part = rows_all[here, lanes].astype(F32) * factor * gain_ref[:, lanes]
            left_t[pl.ds(c * 128, 128), here] = jnp.transpose(part).astype(BF16)

    def give_cov_far(k):
        return remote(
            cov_far.at[pl.ds(k * cov_half, cov_half)],
            cov_relay.at[k],
            cov_sem,
            k,
            dp=dp_next if k == 0 else dp_last,
        )

    def give_cov(k, part):
        where = pl.ds(part * cov_half, cov_half)
        return remote(
            cov_near.at[k, where],
            cov_in.at[k, where],
            cov_sem,
            2 + 2 * k + part,
            dp=dp_next if k == 0 else dp_last,
        )

    def state_relays():
        first_arrived(1, *first_state)
        give_state(5).start()
        first_arrived(2, *first_state)
        give_state(6).start()
        first_arrived(0, *first_state)
        give_state(3).start()
        give_state(4).start()

    def state_relays_on():
        give_state(3).wait_recv()
        give_state(7).start()
        give_state(4).wait_recv()
        give_state(8).start()

        @pl.when(chip < AHEAD + 2)
        def _():
            pass_hidden_on()

    def input_cov():
        def take(slot):
            share_hidden(slot).wait_recv()
            give_inverse(slot).wait_recv()
            fill(
                slot,
                lambda lanes: hidden_in[slot - 1, :, lanes],
                column(inverse_in[slot - 1, 0:1, :]),
            )

        fill(0, lambda lanes: hidden_ref[:, lanes], inverse_all[...])
        take(1)
        take(2)
        take(4)
        give_hidden(7).wait_recv()
        give_hidden(8).wait_recv()
        share_hidden(7).start()
        give_state(5).wait_recv()
        give_state(6).wait_recv()
        take(3)
        take(5)
        take(6)
        give_state(7).wait_recv()
        give_state(8).wait_recv()
        take(7)

        def block(other):
            lanes = pl.ds(pl.multiple_of(other * block_cols, 128), block_cols)
            part = jnp.dot(left_t[...], rows_all[:, lanes], preferred_element_type=F32)
            part = part * gain_ref[:, lanes]
            return jnp.where(odd == 0, part[:block_rows], part[64 : 64 + block_rows])

        cov_far[...] = block((dp + 2) % dps).astype(BF16)
        give_cov_far(0).start()
        give_cov_far(1).start()
        in_cov_ref[...] = block(dp)
        cov_near[0] = block(dp_next).astype(BF16)
        cov_near[1] = block(dp_last).astype(BF16)

    def cov_relays():
        for k in range(2):
            give_cov_far(k).wait_send()
            start(give_cov(k, 1 - k))
        for k in range(2):
            here = pl.ds(k * cov_half, cov_half)
            give_cov_far(k).wait_recv()
            cov_near[k, here, :] = (
                cov_near[k, here, :].astype(F32) + cov_relay[k].astype(F32)
            ).astype(BF16)
            start(give_cov(k, k))

    turn_of = jnp.where(chip > EARLY, sections // CORES - 1 - chip, 3)

    @pl.loop(0, 4)
    def _(phase):
        @pl.when(phase == turn_of)
        def _():
            backward()

        @pl.when(phase == 0)
        def _():
            state_relays()

        @pl.when(phase == 1)
        def _():
            state_relays_on()

        @pl.when(phase == 2)
        def _():
            input_cov()

    cov_relays()

    first_arrived(1, *first_grads)
    start(give_grads(5))
    first_arrived(2, *first_grads)
    start(give_grads(6))
    lend_grads().wait_recv()
    out_rows = out_cov_ref.shape[0]
    for z in range(2):
        lanes = pl.ds(pl.multiple_of(z * (kvw // 2) + (x // 2) * 128, 128), 128)
        for slot in range(3):
            here = pl.ds(slot * rows, rows)
            left_g[z, :, here] = jnp.transpose(grads[here, lanes].astype(F32)).astype(BF16)
    mine = pl.ds(pl.multiple_of((x % 2) * out_rows, 16), out_rows)
    there = pl.ds(0, 3 * rows)
    for z in range(2):
        turned[z] = jnp.dot(left_g[z, mine, there], grads[there, :], preferred_element_type=F32)
    give_grads(5).wait_recv()
    give_grads(6).wait_recv()
    for z in range(2):
        lanes = pl.ds(pl.multiple_of(z * (kvw // 2) + (x // 2) * 128, 128), 128)
        here = pl.ds(3 * rows, rows)
        left_g[z, :, here] = jnp.transpose(grads[here, lanes].astype(F32)).astype(BF16)
        turned[z] += jnp.dot(left_g[z, mine, here], grads[here, :], preferred_element_type=F32)

    def block_of(k):
        z = z_low if k % 2 == 0 else 1 - z_low
        lanes = pl.ds(pl.multiple_of(((dp + k // 2) % dps) * HEAD, 128), HEAD)
        return turned[z, :, lanes]

    def give_out(k):
        return remote(
            out_send.at[k - 1],
            out_recv.at[k - 1],
            out_sem,
            k - 1,
            dp=(dp + k // 2) % dps,
            seq=seq if k % 2 == 0 else z_pair,
        )

    for k in range(1, 2 * dps):
        out_send[k - 1] = block_of(k).astype(BF16)
        start(give_out(k))

    out_cov_ref[...] = block_of(0)
    for k in range(2):
        for part in range(2):
            give_cov(k, part).wait_recv()
    for k in range(1, 2 * dps):
        give_out(k).wait_recv()

    for copy in sent:
        copy.wait_send()
    for slot in (3, 5, 6, 7):
        share_hidden(slot).wait_send()
    for i in (7, 8):
        give_hidden(i).wait_send()
    for i in range(3, 9):
        give_state(i).wait_send()
    for i in (1, 2):
        for layer in range(CORES):
            first_step(i, layer, *first_grads).wait_send()
    lend_grads().wait_send()
    for i in (3, 4):
        give_hidden(i).wait_send()
    share_hidden(4).wait_send()

    @pl.when(dp < halves)
    def _():
        for k in range(1, dps):
            give_fold(k, dp).wait_send()

    @pl.when(has_right)
    def _():
        for i in range(PARTS):
            send_forward(i).wait_send()

    @pl.when(has_left)
    def _():
        for i in range(PARTS):
            send_backward(i).wait_send()


def add_parts(scale, input_own, input_parts, output_own, output_parts, input_cov, output_cov):
    total = input_own[...] + (input_parts[0].astype(F32) + input_parts[1].astype(F32))
    input_cov[...] = total * scale
    total = output_own[...]
    for k in range(output_parts.shape[0]):
        total = total + output_parts[k].astype(F32)
    output_cov[...] = total * scale


def on_device(hidden_in, out_grad, value_weight, norm_gain):
    seqs = lax.axis_size("seq")
    dps = lax.axis_size("dp")
    rows, width = hidden_in.shape[2:]
    window = out_grad.shape[3]
    depth, kvw = value_weight.shape[1:]
    token_count = rows * seqs * dps
    half = rows // CORES
    block = (window // seqs, window // dps)
    out_block = (kvw // seqs, kvw // dps)
    halves = window // depth
    dma = pltpu.SemaphoreType.DMA
    vmem = pl.BlockSpec(memory_space=pltpu.VMEM)
    hbm = pl.BlockSpec(memory_space=pl.ANY)
    scratch = [
        pltpu.VMEM((rows, width), BF16),
        pltpu.VMEM((rows, window), BF16),
        pltpu.VMEM((depth, kvw), BF16),
        pltpu.VMEM((dps - 1, rows, depth), BF16),
        pltpu.VMEM((2, half // 2, depth // CORES), BF16),
        pltpu.VMEM((depth, 128), F32),
        pltpu.VMEM((depth, kvw), BF16),
        pltpu.VMEM((CORES, halves, kvw // halves, kvw), BF16),
        pltpu.VMEM((CORES, kvw, kvw), BF16),
        pltpu.VMEM((rows, kvw), F32),
        pltpu.VMEM((rows, 128), F32),
        pltpu.VMEM((rows, kvw), F32),
        pltpu.VMEM((half, kvw), F32),
        pltpu.VMEM((rows, kvw), BF16),
        pltpu.VMEM((2, half, kvw), BF16),
        pltpu.VMEM((2, rows, kvw), BF16),
        pltpu.VMEM((CORES, 2, half, kvw), BF16),
        pltpu.VMEM((CORES, half, kvw), F32),
        pltpu.VMEM((half, kvw), BF16),
        pltpu.VMEM((half, kvw), BF16),
        pltpu.VMEM((CORES, half, kvw), F32),
        pltpu.VMEM((CORES, half, kvw), F32),
        pltpu.VMEM((CORES, half, 128), F32),
        pltpu.VMEM((CORES, half, kvw), BF16),
        pltpu.VMEM((seqs * rows, kvw), BF16),
        pltpu.VMEM((rows, 128), F32),
        pltpu.VMEM((8, rows), F32),
        pltpu.VMEM((seqs - 1, 8, rows), F32),
        pltpu.VMEM((half, kvw), BF16),
        pltpu.VMEM((half, kvw), BF16),
        pltpu.VMEM((CORES, half, kvw), BF16),
        pltpu.VMEM((RING * rows, kvw), BF16),
        pltpu.VMEM((seqs - 1, rows, window), BF16),
        pltpu.VMEM((seqs * rows, window), BF16),
        pltpu.VMEM((384, seqs * rows), BF16),
        pltpu.VMEM(block, BF16),
        pltpu.VMEM((2, block[0] // 2, block[1]), BF16),
        pltpu.VMEM((2,) + block, BF16),
        pltpu.VMEM((2, 128, RING * rows), BF16),
        pltpu.VMEM((2, kvw // seqs, kvw), F32),
        pltpu.VMEM((2 * dps - 1,) + out_block, BF16),
        dma((3,)),
        dma((2, 2)),
        dma((2, 4)),
        dma((2, 3)),
        dma((2, 3)),
        dma((2, 10)),
        dma((2, dps - 1)),
        dma((2,)),
        dma((2, 2)),
        dma((2, CORES, 2, CORES)),
        dma((2, 2, PARTS)),
        dma((2, 3)),
        dma((2, 9)),
        dma((2, seqs - 1)),
        dma((2, 9)),
        dma((2, 3, CORES)),
        dma((2, seqs - 1)),
        dma((2, 9)),
        dma((2, 3, CORES)),
        dma((2, 6)),
        dma((2, 2 * dps - 1)),
    ]
    input_own, input_parts, output_own, output_parts = pl.pallas_call(
        kernel,
        out_shape=(
            jax.ShapeDtypeStruct(block, F32),
            jax.ShapeDtypeStruct((2,) + block, BF16),
            jax.ShapeDtypeStruct(out_block, F32),
            jax.ShapeDtypeStruct((2 * dps - 1,) + out_block, BF16),
        ),
        in_specs=[hbm, hbm, hbm, vmem],
        out_specs=(vmem,) * 4,
        scratch_shapes=scratch,
        compiler_params=pltpu.CompilerParams(
            collective_id=0, has_side_effects=True, vmem_limit_bytes=56 * 1024 * 1024
        ),
    )(
        hidden_in.reshape(rows, width),
        out_grad.reshape(rows, window),
        value_weight.reshape(depth, kvw),
        norm_gain,
    )
    input_cov, output_cov = pl.pallas_call(
        functools.partial(add_parts, 1.0 / token_count),
        out_shape=(
            jax.ShapeDtypeStruct(block, F32),
            jax.ShapeDtypeStruct(out_block, F32),
        ),
        in_specs=[vmem] * 4,
        out_specs=(vmem,) * 2,
    )(input_own, input_parts, output_own, output_parts)
    return (input_cov[None], output_cov.T[None])


def solution(mesh):
    return jax.shard_map(
        on_device,
        mesh=mesh,
        in_specs=(
            P(None, "dp", "seq", None),
            P(None, "dp", "seq", None),
            P("section", "dp", None),
            P("section", None),
        ),
        out_specs=(P("section", "seq", "dp"), P("section", "dp", "seq")),
        check_vma=False,
    )
```
